256 devices in a mesh: dp: 16 (over x, z_lo), factor: 16 (over z_hi, y, core).
Axes of the slice: x: 4, y: 4, z: 8 (z_hi: 2, z_lo: 4; z = z_hi * 4 + z_lo), core: 2. Of those that a mesh axis runs over, the one named last changes fastest.
Arguments:
- gradients: bfloat16 [16, 128, 512, 512], P('dp', 'factor'), as said below
- old_stats: float32 [16, 16, 512, 512], P('dp', 'factor'), as said below
- owner_table: int32 [16, 16], replicated, may hold values from 0 to 255, as said below
Outputs:
- new_stats: float32 [16, 16, 512, 512], P('dp', 'factor')
- roots: float32 [16, 16, 512, 512], P('dp', 'factor')
The draws below stay inside these ranges and needn't reach their ends.
Inputs may be any that keep to these rules, and one draw needn't show every extreme that they name: `owner_table`: every owner f2 * 16 + d appears exactly once in the table. The 16 owners named by one column have distinct replica indices d, and for every factor index f2 the number of a column's owners with that factor index is 1. Each old_stats[d, f] is symmetric positive definite. `gradients`: gradient partials.
All inputs are finite; a program needn't handle non-finite values.
Results may differ from the reference program's by a relative error of at most 0.0003.
Values may be sent and summed in bfloat16 or wider, within the bound.
A program may use at most 128 MiB of HBM per device.

```python
import math
import jax
import jax.numpy as jnp
from jax import lax

B = 512
ITERS = 5
BLK = 8
N_DP = 16
N_FACTOR = 16


def draw_gradients(key, part):
    key = jax.random.fold_in(key, 11)
    first, second, third = jax.random.split(key, 3)
    shape = (N_DP, BLK * N_FACTOR, B, B)
    row_scales = jnp.exp(jax.random.uniform(first, (1, BLK * N_FACTOR, B, 1), minval=0.0, maxval=math.log(10.0)))
    column_scales = jnp.exp(jax.random.uniform(second, (1, BLK * N_FACTOR, 1, B), minval=0.0, maxval=math.log(10.0)))
    norming = 1.0 / (21.5 * math.sqrt(B * N_DP))
    base = jax.random.normal(third, shape)
    return (base * row_scales * column_scales * norming).astype(jnp.bfloat16)


def draw_old_stats(key, part):
    key = jax.random.fold_in(key, 12)
    first, second, third = jax.random.split(key, 3)
    shape = (N_DP, N_FACTOR, B, 2 * B)
    row_scales = jnp.exp(jax.random.uniform(second, (N_DP, N_FACTOR, B, 1), minval=0.0, maxval=math.log(10.0)))
    base = jax.random.normal(first, shape)
    factors = base * row_scales * math.sqrt(0.11 / (21.5 * 2 * B))
    gram_part = jnp.einsum('dfik,dfjk->dfij', factors, factors, precision=lax.Precision.HIGHEST)
    ridge_spread = jnp.exp(jax.random.uniform(third, (N_DP, N_FACTOR, B), minval=0.0, maxval=math.log(2.0)))
    ridge = 0.03 * ridge_spread * row_scales[..., 0] ** 2
    eye_matrix = jnp.eye(B, dtype=jnp.float32)
    return gram_part + ridge[..., :, None] * eye_matrix


def draw_owner_table(key, part):
    key = jax.random.fold_in(key, 13)
    first, second, third, fourth = jax.random.split(key, 4)
    quota = N_DP // N_FACTOR
    columns = jnp.arange(N_FACTOR, dtype=jnp.int32)[:, None]
    slots = jnp.arange(N_DP, dtype=jnp.int32)[None, :]
    base_factor = (columns + slots // quota) % N_FACTOR
    base_replica = jnp.broadcast_to(slots, (N_FACTOR, N_DP))
    replica_labels = jax.random.permutation(first, N_DP).astype(jnp.int32)
    factor_labels = jax.random.permutation(second, N_FACTOR).astype(jnp.int32)
    replicas = jnp.take(replica_labels, base_replica)
    factors = jnp.take(factor_labels, base_factor)
    table = factors * N_DP + replicas
    column_order = jax.random.permutation(third, N_FACTOR).astype(jnp.int32)
    table = jnp.take(table, column_order, axis=0)
    row_keys = jax.random.split(fourth, N_FACTOR)
    shuffles = jax.vmap(lambda k: jax.random.permutation(k, N_DP).astype(jnp.int32))(row_keys)
    table = jnp.take_along_axis(table, shuffles, axis=1)
    return table.astype(jnp.int32)


def setup_inputs(seed: int = 0) -> dict:
    seeds = jax.random.split(jax.random.key(seed), 4)
    gradients = draw_gradients(jax.random.fold_in(seeds[3], 71), 0)
    old_stats = draw_old_stats(jax.random.fold_in(seeds[3], 71), 0)
    owner_table = draw_owner_table(jax.random.fold_in(seeds[3], 71), 0)
    return dict(gradients=gradients, old_stats=old_stats, owner_table=owner_table)


BETA = 0.9
HIGHEST = lax.Precision.HIGHEST

def block_gram(blocks, side):
    wide = blocks.astype(jnp.float32)
    chosen = jnp.where(side == 1, jnp.swapaxes(wide, 1, 2), wide)
    return jnp.einsum('rik,rjk->ij', chosen, chosen, precision=HIGHEST)

def inverse_root(stats):
    eye_matrix = jnp.eye(stats.shape[0], dtype=jnp.float32)
    scale = 2.5 / jnp.sqrt(jnp.sum(stats * stats) + 1e-06)
    moving = scale * stats
    root = eye_matrix
    for sweep in range(ITERS):
        factor = 1.25 * eye_matrix - 0.25 * moving
        root = jnp.dot(root, factor, precision=HIGHEST)
        square = jnp.dot(factor, factor, precision=HIGHEST)
        fourth = jnp.dot(square, square, precision=HIGHEST)
        moving = jnp.dot(fourth, moving, precision=HIGHEST)
    return jnp.sqrt(jnp.sqrt(scale)) * root

def reference(gradients, old_stats, owner_table):
    flat_table = owner_table.reshape(-1).astype(jnp.int32)
    positions = jnp.arange(flat_table.shape[0], dtype=jnp.int32)

    def one_owner(index):
        replica = index // N_FACTOR
        owner_column = index % N_FACTOR
        target = owner_column * N_DP + replica
        source = jnp.sum(jnp.where(flat_table == target, positions, 0)).astype(jnp.int32)
        column = source // N_DP
        matrix = source % N_DP
        block_index = (column * BLK + matrix // 2).astype(jnp.int32)
        blocks = lax.dynamic_index_in_dim(gradients, block_index, 1, keepdims=False)
        gram = block_gram(blocks, matrix % 2)
        previous = old_stats[replica, owner_column]
        stats = BETA * previous + (1.0 - BETA) * gram
        return (stats, inverse_root(stats))
    stats, roots = lax.map(one_owner, jnp.arange(N_DP * N_FACTOR, dtype=jnp.int32))
    return (stats.reshape(N_DP, N_FACTOR, B, B), roots.reshape(N_DP, N_FACTOR, B, B))
```

```python
import jax
import jax.numpy as jnp
from jax import lax
from jax.experimental import pallas as pl
from jax.experimental.pallas import tpu as pltpu
from jax.sharding import PartitionSpec as P

ITERS = 5
BETA = 0.9
B = 512
T = 128
MESH = pl.DeviceIdType.MESH
TILES = ((0, 0), (0, 1), (1, 1), (0, 2), (0, 3), (1, 2), (1, 3), (2, 2), (2, 3), (3, 3))
NT = len(TILES)
QUADS = ((0, 0), (0, 1), (1, 1))


def route(items_ref, columns_ref, grads, out, xg, part, r1, r2, xt, fs, fr, ds, dr,
          own_sem, xs, xr, zs, zr, ts, tr, as_, ar, bs, br):
    d = lax.axis_index("dp")
    f = lax.axis_index("factor")
    x, zl = d // 4, d % 4
    zh = f // 8
    q = zl + zh * (3 - 2 * zl)
    b0, b1 = q % 2, q // 2
    home = b0 * 8 + b1 * 4

    def dp_at(x_, q_, zh_):
        return x_ * 4 + q_ + zh_ * (3 - 2 * q_)

    def x_peer(k):
        return {"dp": dp_at((x + k) % 4, q, zh), "factor": f}

    def z_peer(step):
        flip = q + 1 - 2 * b0 if step == 0 else q + 2 - 4 * b1
        return {"dp": dp_at(x, flip, zh), "factor": f}

    def f_peer(g):
        return {"dp": dp_at(x, q, g // 8), "factor": g}

    def d_peer(e):
        return {"dp": e, "factor": f}

    barrier = pltpu.get_barrier_semaphore()
    for k in range(1, 16):
        pl.semaphore_signal(barrier, inc=1, device_id=d_peer((d + k) % 16), device_id_type=MESH)
        pl.semaphore_signal(barrier, inc=1, device_id=f_peer((f + k) % 16), device_id_type=MESH)
    own = [pltpu.make_async_copy(grads.at[2 * x + c], xg.at[c, 0], own_sem.at[c]) for c in range(2)]
    for copy in own:
        copy.start()
    pl.semaphore_wait(barrier, 30)

    def x_copy(c, k):
        return pltpu.make_async_remote_copy(
            src_ref=grads.at[2 * ((x + k) % 4) + c], dst_ref=xg.at[c, k],
            send_sem=xs.at[c, k], recv_sem=xr.at[c, k], device_id=x_peer(k), device_id_type=MESH)

    def z_copy(c, step):
        if step == 0:
            src, dst = part.at[c, pl.ds((1 - b0) * 8, 8)], r1.at[c]
        else:
            src, dst = part.at[c, pl.ds(b0 * 8 + (1 - b1) * 4, 4)], r2.at[c]
        return pltpu.make_async_remote_copy(
            src_ref=src, dst_ref=dst, send_sem=zs.at[c, step], recv_sem=zr.at[c, step],
            device_id=z_peer(step), device_id_type=MESH)

    def t_copy(c, k):
        return pltpu.make_async_remote_copy(
            src_ref=part.at[c, home + (x + k) % 4], dst_ref=xt.at[pl.ds(4 * x + 2 * c, 2)],
            send_sem=ts.at[c, k], recv_sem=tr.at[c, k], device_id=x_peer(k), device_id_type=MESH)

    def a_copy(g):
        return pltpu.make_async_remote_copy(
            src_ref=fs.at[g], dst_ref=fr.at[f], send_sem=as_.at[g], recv_sem=ar.at[f],
            device_id=f_peer(g), device_id_type=MESH)

    def a_landed(g):
        return pltpu.make_async_remote_copy(
            src_ref=fs.at[g], dst_ref=fr.at[g], send_sem=as_.at[g], recv_sem=ar.at[g],
            device_id=f_peer(g), device_id_type=MESH)

    piece = home + x

    def b_copy(e):
        return pltpu.make_async_remote_copy(
            src_ref=ds.at[e], dst_ref=dr.at[piece], send_sem=bs.at[e], recv_sem=br.at[piece],
            device_id=d_peer(e), device_id_type=MESH)

    def b_landed(e):
        e_x, e_zl = e // 4, e % 4
        e_q = e_zl + zh * (3 - 2 * e_zl)
        e_piece = (e_q % 2) * 8 + (e_q // 2) * 4 + e_x
        return pltpu.make_async_remote_copy(
            src_ref=ds.at[e], dst_ref=dr.at[e_piece], send_sem=bs.at[e], recv_sem=br.at[e_piece],
            device_id=d_peer(e), device_id_type=MESH)

    def grams(c):
        for side in range(2):
            for row, col in QUADS:
                total = None
                for k in range(4):
                    if side == 0:
                        left = xg[c, k, row * 256:(row + 1) * 256, :]
                        right = xg[c, k, col * 256:(col + 1) * 256, :]
                        dims = (((1,), (1,)), ((), ()))
                    else:
                        left = xg[c, k, :, row * 256:(row + 1) * 256]
                        right = xg[c, k, :, col * 256:(col + 1) * 256]
                        dims = (((0,), (0,)), ((), ()))
                    term = lax.dot_general(left, right, dims, preferred_element_type=jnp.float32)
                    total = term if total is None else total + term
                for n, (i, j) in enumerate(TILES):
                    if i // 2 == row and j // 2 == col:
                        i0, j0 = (i % 2) * T, (j % 2) * T
                        part[c, :, side, n] = total[i0:i0 + T, j0:j0 + T].reshape(16, 8, T)

    def fold(c, step):
        if step == 0:
            part[c, pl.ds(b0 * 8, 8)] += r1[c]
        else:
            part[c, pl.ds(home, 4)] += r2[c]

    def spread(c):
        for k in (2, 1, 3):
            t_copy(c, k).start()
        xt[pl.ds(4 * x + 2 * c, 2)] = part[c, home + x]

    order = (2, 1, 3)
    for k in order:
        x_copy(0, k).start()
    for k in order:
        x_copy(0, k).wait_send()
    for k in order:
        x_copy(1, k).start()
    own[0].wait()
    for k in order:
        x_copy(0, k).wait_recv()
    grams(0)
    z_copy(0, 0).start()
    z_copy(0, 0).wait_recv()
    fold(0, 0)
    z_copy(0, 1).start()
    own[1].wait()
    for k in order:
        x_copy(1, k).wait_recv()
    grams(1)
    z_copy(1, 0).start()
    z_copy(0, 1).wait_recv()
    fold(0, 1)
    spread(0)
    z_copy(1, 0).wait_recv()
    fold(1, 0)
    z_copy(1, 1).start()
    z_copy(1, 1).wait_recv()
    fold(1, 1)
    spread(1)
    for c in range(2):
        for k in order:
            t_copy(c, k).wait_recv()

    for k in range(1, 16):
        g = (f + k) % 16
        fs[g] = xt[items_ref[g]]
        a_copy(g).start()
    fr[f] = xt[items_ref[f]]
    for k in range(1, 16):
        a_landed((f + k) % 16).wait_recv()
    for k in range(1, 16):
        e = (d + k) % 16
        ds[e] = fr[columns_ref[e]]
        b_copy(e).start()
    dr[piece] = fr[columns_ref[d]]
    for k in range(1, 16):
        b_landed((d + k) % 16).wait_recv()
    out[...] = dr[...]

    for k in order:
        x_copy(1, k).wait_send()
    for c in range(2):
        for step in range(2):
            z_copy(c, step).wait_send()
        for k in order:
            t_copy(c, k).wait_send()
    for k in range(1, 16):
        a_copy((f + k) % 16).wait_send()
        b_copy((d + k) % 16).wait_send()


def routed(items, columns, grads):
    tile = (NT, 8, T)
    return pl.pallas_call(
        route,
        out_shape=jax.ShapeDtypeStruct((16,) + tile, jnp.float32),
        in_specs=[
            pl.BlockSpec(memory_space=pltpu.SMEM),
            pl.BlockSpec(memory_space=pltpu.SMEM),
            pl.BlockSpec(memory_space=pl.ANY),
        ],
        out_specs=pl.BlockSpec(memory_space=pltpu.VMEM),
        scratch_shapes=[
            pltpu.VMEM((2, 4, B, B), jnp.bfloat16),
            pltpu.VMEM((2, 16, 2) + tile, jnp.float32),
            pltpu.VMEM((2, 8, 2) + tile, jnp.float32),
            pltpu.VMEM((2, 4, 2) + tile, jnp.float32),
            pltpu.VMEM((16,) + tile, jnp.float32),
            pltpu.VMEM((16,) + tile, jnp.float32),
            pltpu.VMEM((16,) + tile, jnp.float32),
            pltpu.VMEM((16,) + tile, jnp.float32),
            pltpu.VMEM((16,) + tile, jnp.float32),
            pltpu.SemaphoreType.DMA((2,)),
            pltpu.SemaphoreType.DMA((2, 4)),
            pltpu.SemaphoreType.DMA((2, 4)),
            pltpu.SemaphoreType.DMA((2, 2)),
            pltpu.SemaphoreType.DMA((2, 2)),
            pltpu.SemaphoreType.DMA((2, 4)),
            pltpu.SemaphoreType.DMA((2, 4)),
            pltpu.SemaphoreType.DMA((16,)),
            pltpu.SemaphoreType.DMA((16,)),
            pltpu.SemaphoreType.DMA((16,)),
            pltpu.SemaphoreType.DMA((16,)),
        ],
        compiler_params=pltpu.CompilerParams(
            collective_id=0, has_side_effects=True, vmem_limit_bytes=48 * 1024 * 1024
        ),
        cost_estimate=pl.CostEstimate(flops=4 * 10**9, bytes_accessed=8 * 10**6, transcendentals=0),
        name="route",
    )(items, columns, grads)


def split(a):
    high = a.astype(jnp.bfloat16)
    return high, (a - high.astype(jnp.float32)).astype(jnp.bfloat16)


def product(a, b):
    def dot(left, right):
        return jnp.dot(left, right, preferred_element_type=jnp.float32)

    return dot(a[0], b[0]) + (dot(a[0], b[1]) + dot(a[1], b[0]))


def newton(tri, old, stats, roots, moving, root):
    for n, (i, j) in enumerate(TILES):
        block = tri[:, n].reshape(T, T)
        rows, cols = slice(i * T, (i + 1) * T), slice(j * T, (j + 1) * T)
        stats[rows, cols] = BETA * old[rows, cols] + (1.0 - BETA) * block
        if i != j:
            stats[cols, rows] = BETA * old[cols, rows] + (1.0 - BETA) * block.T
    scale = 2.5 / jnp.sqrt(jnp.sum(stats[...] * stats[...], keepdims=True) + 1e-06)
    eye = (lax.broadcasted_iota(jnp.int32, (B, B), 0) == lax.broadcasted_iota(jnp.int32, (B, B), 1))

    def factor_of(m):
        return jnp.where(eye, 1.25, 0.0) - 0.25 * m

    def advance(factor, m):
        square = split(product(factor, factor))
        fourth = split(product(square, square))
        moving[...] = product(fourth, split(m))

    m = scale * stats[...]
    first = factor_of(m)
    root[...] = first
    advance(split(first), m)

    def sweep(_, carry):
        m = moving[...]
        factor = split(factor_of(m))
        root[...] = product(split(root[...]), factor)
        advance(factor, m)
        return carry

    lax.fori_loop(0, ITERS - 2, sweep, 0)
    last = product(split(root[...]), split(factor_of(moving[...])))
    roots[...] = jnp.sqrt(jnp.sqrt(scale)) * last


def finished(tri, old):
    whole = pl.BlockSpec(memory_space=pltpu.VMEM)
    return pl.pallas_call(
        newton,
        out_shape=(jax.ShapeDtypeStruct((B, B), jnp.float32),) * 2,
        in_specs=[whole, whole],
        out_specs=(whole, whole),
        scratch_shapes=[pltpu.VMEM((B, B), jnp.float32)] * 2,
        compiler_params=pltpu.CompilerParams(vmem_limit_bytes=48 * 1024 * 1024),
        cost_estimate=pl.CostEstimate(flops=13 * 10**9, bytes_accessed=4 * 10**6, transcendentals=0),
        name="newton",
    )(tri, old)


def local(gradients, old_stats, owner_table):
    f = lax.axis_index("factor")
    slots = jnp.arange(16, dtype=jnp.int32)
    mine = lax.dynamic_index_in_dim(owner_table, f, 0, keepdims=False)
    items = jnp.sum(jnp.where(mine[None, :] // 16 == slots[:, None], slots[None, :], 0), axis=1)
    wanted = (owner_table[None] == f * 16 + slots[:, None, None])
    columns = jnp.sum(jnp.where(wanted, slots[None, :, None], 0), axis=(1, 2))
    tri = routed(items, columns, gradients[0])
    stats, roots = finished(tri, old_stats[0, 0])
    return (stats[None, None], roots[None, None])


def solution(mesh):
    placed = (P("dp", "factor", None, None), P("dp", "factor", None, None), P())
    return jax.shard_map(
        local,
        mesh=mesh,
        in_specs=placed,
        out_specs=(P("dp", "factor", None, None), P("dp", "factor", None, None)),
        check_vma=False,
    )
```

```python
import jax
import jax.numpy as jnp
from jax import lax
from jax.experimental import pallas as pl
from jax.experimental.pallas import tpu as pltpu
from jax.sharding import PartitionSpec as P

ITERS = 5
BETA = 0.9
B = 512
T = 128
MESH = pl.DeviceIdType.MESH
TILES = ((0, 1), (0, 2), (0, 3), (1, 2), (1, 3), (2, 3), (0, 0), (1, 1), (2, 2))
NT = len(TILES)
H = 256
QUADS = ((1, 1), (0, 0), (0, 1))


def low_left():
    rows = lax.broadcasted_iota(jnp.int32, (T, T), 0)
    cols = lax.broadcasted_iota(jnp.int32, (T, T), 1)
    return jnp.logical_and(rows >= T // 2, cols < T // 2)


def swapped(block):
    return jnp.concatenate([block[T // 2:], block[:T // 2]], axis=0)


def turned(block):
    return jnp.concatenate([block[:, T // 2:], block[:, :T // 2]], axis=1)


def route(table, grads, out, xg, part, r1, r2, xt, fs, fr, ds, dr, items, columns,
          own_sem, xs, xr, zs, zr, ts, tr, as_, ar, bs, br, turn):
    d = lax.axis_index("dp")
    f = lax.axis_index("factor")
    x, zl = d // 4, d % 4
    zh, core = f // 8, f % 2
    q = zl + zh * (3 - 2 * zl)
    b0, b1 = q % 2, q // 2
    home = b0 * 8 + b1 * 4
    piece = home + x

    def dp_at(x_, q_, zh_):
        return x_ * 4 + q_ + zh_ * (3 - 2 * q_)

    def x_peer(k):
        return {"dp": dp_at((x + k) % 4, q, zh), "factor": f}

    def z_peer(step):
        flip = q + 1 - 2 * b0 if step == 0 else q + 2 - 4 * b1
        return {"dp": dp_at(x, flip, zh), "factor": f}

    def f_peer(g):
        return {"dp": dp_at(x, q, g // 8), "factor": g}

    def d_peer(e):
        return {"dp": e, "factor": f}

    barrier = pltpu.get_barrier_semaphore()
    for k in range(1, 16):
        pl.semaphore_signal(barrier, inc=1, device_id=d_peer((d + k) % 16), device_id_type=MESH)
        pl.semaphore_signal(barrier, inc=1, device_id=f_peer((f + k) % 16), device_id_type=MESH)
    own = [pltpu.make_async_copy(grads.at[2 * x + c], xg.at[c, 0], own_sem.at[c]) for c in range(2)]
    for copy in own:
        copy.start()

    owners = [table[f, j] for j in range(16)]
    for g in range(16):
        pick = jnp.int32(0)
        for j in range(16):
            pick = jnp.where(lax.shift_right_logical(owners[j], 4) == g, j, pick)
        items[g] = pick

    def find_column(e, carry):
        def scan(c, found):
            for j in range(16):
                found = jnp.where(table[c, j] == f * 16 + e, c, found)
            return found
        columns[e] = lax.fori_loop(0, 16, scan, jnp.int32(0))
        return carry

    pl.semaphore_wait(barrier, 30)

    def x_copy(c, k):
        return pltpu.make_async_remote_copy(
            src_ref=grads.at[2 * ((x + k) % 4) + c], dst_ref=xg.at[c, k],
            send_sem=xs.at[c, k], recv_sem=xr.at[c, k], device_id=x_peer(k), device_id_type=MESH)

    def z_copy(c, side, step):
        if step == 0:
            src, dst = part.at[c, side, pl.ds((1 - b0) * 8, 8)], r1.at[c, side]
        else:
            src, dst = part.at[c, side, pl.ds(b0 * 8 + (1 - b1) * 4, 4)], r2.at[c, side]
        return pltpu.make_async_remote_copy(
            src_ref=src, dst_ref=dst, send_sem=zs.at[c, side, step], recv_sem=zr.at[c, side, step],
            device_id=z_peer(step), device_id_type=MESH)

    def t_copy(c, side, k):
        return pltpu.make_async_remote_copy(
            src_ref=part.at[c, side, home + (x + k) % 4], dst_ref=xt.at[4 * x + 2 * c + side],
            send_sem=ts.at[c, side, k], recv_sem=tr.at[c, side, k], device_id=x_peer(k), device_id_type=MESH)

    def a_copy(g):
        return pltpu.make_async_remote_copy(
            src_ref=fs.at[g], dst_ref=fr.at[f], send_sem=as_.at[g], recv_sem=ar.at[f],
            device_id=f_peer(g), device_id_type=MESH)

    def a_landed(g):
        return pltpu.make_async_remote_copy(
            src_ref=fs.at[g], dst_ref=fr.at[g], send_sem=as_.at[g], recv_sem=ar.at[g],
            device_id=f_peer(g), device_id_type=MESH)

    def b_copy(e):
        return pltpu.make_async_remote_copy(
            src_ref=ds.at[e], dst_ref=dr.at[piece], send_sem=bs.at[e], recv_sem=br.at[piece],
            device_id=d_peer(e), device_id_type=MESH)

    def b_landed(e):
        e_x, e_zl = e // 4, e % 4
        e_q = e_zl + zh * (3 - 2 * e_zl)
        e_piece = (e_q % 2) * 8 + (e_q // 2) * 4 + e_x
        return pltpu.make_async_remote_copy(
            src_ref=ds.at[e], dst_ref=dr.at[e_piece], send_sem=bs.at[e], recv_sem=br.at[e_piece],
            device_id=d_peer(e), device_id_type=MESH)

    def gram(c, side):
        corner = None
        corner_parts = ()
        for row, col in QUADS:
            total = None
            for k in range(4):
                if side == 0:
                    left = xg[c, k, row * H:(row + 1) * H, :]
                    right = xg[c, k, col * H:(col + 1) * H, :]
                    dims = (((1,), (1,)), ((), ()))
                else:
                    left = xg[c, k, :, row * H:(row + 1) * H]
                    right = xg[c, k, :, col * H:(col + 1) * H]
                    dims = (((0,), (0,)), ((), ()))
                term = lax.dot_general(left, right, dims, preferred_element_type=jnp.float32)
                total = term if total is None else total + term
            if corner is None:
                corner = total[T:, T:]
                shifted = swapped(corner)
                corner_parts = (shifted, turned(shifted), turned(corner))
            for n, (i, j) in enumerate(TILES):
                if i // 2 == row and j // 2 == col:
                    i0, j0 = (i % 2) * T, (j % 2) * T
                    block = total[i0:i0 + T, j0:j0 + T]
                    if i == j:
                        block = jnp.where(low_left(), corner_parts[i], block)
                    part[c, side, :, n] = block.reshape(16, 8, T)

    def fold(c, side, step):
        if step == 0:
            part[c, side, pl.ds(b0 * 8, 8)] += r1[c, side]
        else:
            part[c, side, pl.ds(home, 4)] += r2[c, side]

    def spread(c, side):
        for k in order:
            t_copy(c, side, k).start()
        xt[4 * x + 2 * c + side] = part[c, side, piece]

    order = (2, 1, 3)

    def send_x():
        for c in range(2):
            for k in order:
                x_copy(c, k).start()
            for k in order:
                x_copy(c, k).wait_send()

    @pl.when(core == 0)
    def _():
        send_x()
        pl.semaphore_signal(turn, inc=1, device_id={"dp": d, "factor": f + 1}, device_id_type=MESH)

    @pl.when(core == 1)
    def _():
        pl.semaphore_wait(turn, 1)
        send_x()

    lax.fori_loop(0, 16, find_column, 0)

    def arrive(c):
        own[c].wait()
        for k in order:
            x_copy(c, k).wait_recv()
        for side in range(2):
            gram(c, side)
            z_copy(c, side, 0).start()

    def halve(c):
        for side in range(2):
            z_copy(c, side, 0).wait_recv()
            fold(c, side, 0)
            z_copy(c, side, 1).start()

    def settle(c):
        for side in range(2):
            z_copy(c, side, 1).wait_recv()
            fold(c, side, 1)
            spread(c, side)

    arrive(0)
    halve(0)
    arrive(1)
    settle(0)
    halve(1)
    settle(1)
    for c in range(2):
        for side in range(2):
            for k in order:
                t_copy(c, side, k).wait_recv()

    for k in range(1, 16):
        g = (f + k) % 16
        fs[g] = xt[items[g]]
        a_copy(g).start()
    fr[f] = xt[items[f]]
    for k in range(1, 16):
        a_landed((f + k) % 16).wait_recv()
    for k in range(1, 16):
        e = (d + k) % 16
        ds[e] = fr[columns[e]]
        b_copy(e).start()
    dr[piece] = fr[columns[d]]
    for k in range(1, 16):
        b_landed((d + k) % 16).wait_recv()
    out[...] = dr[...]

    for c in range(2):
        for side in range(2):
            for step in range(2):
                z_copy(c, side, step).wait_send()
            for k in order:
                t_copy(c, side, k).wait_send()
    for k in range(1, 16):
        a_copy((f + k) % 16).wait_send()
        b_copy((d + k) % 16).wait_send()


def routed(table, grads):
    tile = (NT, 8, T)
    return pl.pallas_call(
        route,
        out_shape=jax.ShapeDtypeStruct((16,) + tile, jnp.float32),
        in_specs=[
            pl.BlockSpec(memory_space=pltpu.SMEM),
            pl.BlockSpec(memory_space=pltpu.HBM),
        ],
        out_specs=pl.BlockSpec(memory_space=pltpu.VMEM),
        scratch_shapes=[
            pltpu.VMEM((2, 4, B, B), jnp.bfloat16),
            pltpu.VMEM((2, 2, 16) + tile, jnp.float32),
            pltpu.VMEM((2, 2, 8) + tile, jnp.float32),
            pltpu.VMEM((2, 2, 4) + tile, jnp.float32),
            pltpu.VMEM((16,) + tile, jnp.float32),
            pltpu.VMEM((16,) + tile, jnp.float32),
            pltpu.VMEM((16,) + tile, jnp.float32),
            pltpu.VMEM((16,) + tile, jnp.float32),
            pltpu.VMEM((16,) + tile, jnp.float32),
            pltpu.SMEM((16,), jnp.int32),
            pltpu.SMEM((16,), jnp.int32),
            pltpu.SemaphoreType.DMA((2,)),
            pltpu.SemaphoreType.DMA((2, 4)),
            pltpu.SemaphoreType.DMA((2, 4)),
            pltpu.SemaphoreType.DMA((2, 2, 2)),
            pltpu.SemaphoreType.DMA((2, 2, 2)),
            pltpu.SemaphoreType.DMA((2, 2, 4)),
            pltpu.SemaphoreType.DMA((2, 2, 4)),
            pltpu.SemaphoreType.DMA((16,)),
            pltpu.SemaphoreType.DMA((16,)),
            pltpu.SemaphoreType.DMA((16,)),
            pltpu.SemaphoreType.DMA((16,)),
            pltpu.SemaphoreType.REGULAR,
        ],
        compiler_params=pltpu.CompilerParams(
            collective_id=0, has_side_effects=True, vmem_limit_bytes=60 * 1024 * 1024
        ),
        cost_estimate=pl.CostEstimate(flops=4 * 10**9, bytes_accessed=8 * 10**6, transcendentals=0),
        name="route",
    )(table, grads)


def split(a):
    high = a.astype(jnp.bfloat16)
    return high, (a - high.astype(jnp.float32)).astype(jnp.bfloat16)


def dot(left, right):
    return jnp.dot(left, right, preferred_element_type=jnp.float32)


def product(a, b):
    def quad(r, c):
        rows, cols = slice(r * H, (r + 1) * H), slice(c * H, (c + 1) * H)
        return dot(a[0][rows], b[0][:, cols]) + (dot(a[0][rows], b[1][:, cols]) + dot(a[1][rows], b[0][:, cols]))

    upper = quad(0, 1)
    top = jnp.concatenate([quad(0, 0), upper], axis=1)
    return jnp.concatenate([top, jnp.concatenate([upper.T, quad(1, 1)], axis=1)], axis=0)


def newton(tri, old, stats, roots, moving, root):
    def blend(i, j, block):
        rows, cols = slice(i * T, (i + 1) * T), slice(j * T, (j + 1) * T)
        stats[rows, cols] = BETA * old[rows, cols] + (1.0 - BETA) * block

    mask = low_left()
    kept = []
    for n, (i, j) in enumerate(TILES):
        block = tri[:, n].reshape(T, T)
        if i == j:
            kept.append(block)
            blend(i, i, jnp.where(mask, block.T, block))
        else:
            blend(i, j, block)
            blend(j, i, block.T)
    first, second, third = kept
    left = lax.broadcasted_iota(jnp.int32, (T // 2, T), 1) < T // 2
    top = jnp.where(left, first[T // 2:], turned(second[T // 2:]))
    corner = jnp.concatenate([top, turned(third[T // 2:])], axis=0)
    blend(3, 3, jnp.where(mask, corner.T, corner))

    scale = 2.5 / jnp.sqrt(jnp.sum(stats[...] * stats[...], keepdims=True) + 1e-06)
    eye = (lax.broadcasted_iota(jnp.int32, (B, B), 0) == lax.broadcasted_iota(jnp.int32, (B, B), 1))

    def factor_of(m):
        return jnp.where(eye, 1.25, 0.0) - 0.25 * m

    def advance(factor, m):
        square = split(product(factor, factor))
        fourth = split(product(square, square))
        moving[...] = product(fourth, split(m))

    m = scale * stats[...]
    start = factor_of(m)
    root[...] = start
    advance(split(start), m)

    def sweep(_, carry):
        m = moving[...]
        factor = split(factor_of(m))
        root[...] = product(split(root[...]), factor)
        advance(factor, m)
        return carry

    lax.fori_loop(0, ITERS - 2, sweep, 0)
    last = product(split(root[...]), split(factor_of(moving[...])))
    roots[...] = jnp.sqrt(jnp.sqrt(scale)) * last


def finished(tri, old):
    whole = pl.BlockSpec(memory_space=pltpu.VMEM)
    return pl.pallas_call(
        newton,
        out_shape=(jax.ShapeDtypeStruct((B, B), jnp.float32),) * 2,
        in_specs=[whole, whole],
        out_specs=(whole, whole),
        scratch_shapes=[pltpu.VMEM((B, B), jnp.float32)] * 2,
        compiler_params=pltpu.CompilerParams(vmem_limit_bytes=48 * 1024 * 1024),
        cost_estimate=pl.CostEstimate(flops=13 * 10**9, bytes_accessed=4 * 10**6, transcendentals=0),
        name="newton",
    )(tri, old)


def local(gradients, old_stats, owner_table):
    tri = routed(owner_table, gradients[0])
    stats, roots = finished(tri, old_stats[0, 0])
    return (stats[None, None], roots[None, None])


def solution(mesh):
    placed = (P("dp", "factor", None, None), P("dp", "factor", None, None), P())
    return jax.shard_map(
        local,
        mesh=mesh,
        in_specs=placed,
        out_specs=(P("dp", "factor", None, None), P("dp", "factor", None, None)),
        check_vma=False,
    )
```

```python
import jax
import jax.numpy as jnp
from jax import lax
from jax.experimental import pallas as pl
from jax.experimental.pallas import tpu as pltpu
from jax.sharding import PartitionSpec as P

ITERS = 5
BETA = 0.9
B = 512
T = 128
MESH = pl.DeviceIdType.MESH
TILES = ((0, 1), (0, 2), (0, 3), (1, 2), (1, 3), (2, 3), (0, 0), (1, 1), (2, 2))
NT = len(TILES)
H = 256
QUADS = ((1, 1), (0, 0), (0, 1))


def low_left():
    rows = lax.broadcasted_iota(jnp.int32, (T, T), 0)
    cols = lax.broadcasted_iota(jnp.int32, (T, T), 1)
    return jnp.logical_and(rows >= T // 2, cols < T // 2)


def swapped(block):
    return jnp.concatenate([block[T // 2:], block[:T // 2]], axis=0)


def turned(block):
    return jnp.concatenate([block[:, T // 2:], block[:, :T // 2]], axis=1)


def route(table, grads, out, xg, part, r1, r2, r3, xt, fs, fr, ds, dr, items, columns,
          own_sem, xs, xr, zs, zr, ws, wr, ts, tr, as_, ar, bs, br, turn):
    d = lax.axis_index("dp")
    f = lax.axis_index("factor")
    x, zl = d // 4, d % 4
    zh, core = f // 8, f % 2
    q = zl + zh * (3 - 2 * zl)
    b0, b1 = q % 2, q // 2
    home = b0 * 8 + b1 * 4
    piece = home + x

    def dp_at(x_, q_, zh_):
        return x_ * 4 + q_ + zh_ * (3 - 2 * q_)

    def x_peer(k):
        return {"dp": dp_at((x + k) % 4, q, zh), "factor": f}

    def z_peer(step):
        flip = q + 1 - 2 * b0 if step == 0 else q + 2 - 4 * b1
        return {"dp": dp_at(x, flip, zh), "factor": f}

    def f_peer(g):
        return {"dp": dp_at(x, q, g // 8), "factor": g}

    def d_peer(e):
        return {"dp": e, "factor": f}

    barrier = pltpu.get_barrier_semaphore()
    for k in range(1, 16):
        pl.semaphore_signal(barrier, inc=1, device_id=d_peer((d + k) % 16), device_id_type=MESH)
        pl.semaphore_signal(barrier, inc=1, device_id=f_peer((f + k) % 16), device_id_type=MESH)
    own = [pltpu.make_async_copy(grads.at[2 * x + c], xg.at[c, 0], own_sem.at[c]) for c in range(2)]
    for copy in own:
        copy.start()

    def find_column(e, carry):
        def scan(c, found):
            for j in range(16):
                found = jnp.where(table[c, j] == f * 16 + e, c, found)
            return found
        columns[e] = lax.fori_loop(0, 16, scan, jnp.int32(0))
        return carry

    pl.semaphore_wait(barrier, 30)

    def x_copy(c, k):
        return pltpu.make_async_remote_copy(
            src_ref=grads.at[2 * ((x + k) % 4) + c], dst_ref=xg.at[c, k],
            send_sem=xs.at[c, k], recv_sem=xr.at[c, k], device_id=x_peer(k), device_id_type=MESH)

    def z_copy(c, side, step):
        if step == 0:
            src, dst = part.at[c, side, pl.ds((1 - b0) * 8, 8)], r1.at[side]
        else:
            src, dst = part.at[c, side, pl.ds(b0 * 8 + (1 - b1) * 4, 4)], r2.at[side]
        return pltpu.make_async_remote_copy(
            src_ref=src, dst_ref=dst, send_sem=zs.at[side, step], recv_sem=zr.at[side, step],
            device_id=z_peer(step), device_id_type=MESH)

    def w_copy(side, k):
        to = (q + k) % 4
        return pltpu.make_async_remote_copy(
            src_ref=part.at[1, side, pl.ds((to % 2) * 8 + (to // 2) * 4, 4)], dst_ref=r3.at[side, k],
            send_sem=ws.at[side, k], recv_sem=wr.at[side, k],
            device_id={"dp": dp_at(x, to, zh), "factor": f}, device_id_type=MESH)

    def t_copy(c, side, k):
        return pltpu.make_async_remote_copy(
            src_ref=part.at[c, side, home + (x + k) % 4], dst_ref=xt.at[4 * x + 2 * c + side],
            send_sem=ts.at[c, side, k], recv_sem=tr.at[c, side, k], device_id=x_peer(k), device_id_type=MESH)

    def a_copy(g):
        return pltpu.make_async_remote_copy(
            src_ref=fs.at[g], dst_ref=fr.at[f], send_sem=as_.at[g], recv_sem=ar.at[f],
            device_id=f_peer(g), device_id_type=MESH)

    def a_landed(g):
        return pltpu.make_async_remote_copy(
            src_ref=fs.at[g], dst_ref=fr.at[g], send_sem=as_.at[g], recv_sem=ar.at[g],
            device_id=f_peer(g), device_id_type=MESH)

    def b_copy(e):
        return pltpu.make_async_remote_copy(
            src_ref=ds.at[e], dst_ref=dr.at[piece], send_sem=bs.at[e], recv_sem=br.at[piece],
            device_id=d_peer(e), device_id_type=MESH)

    def b_landed(e):
        e_x, e_zl = e // 4, e % 4
        e_q = e_zl + zh * (3 - 2 * e_zl)
        e_piece = (e_q % 2) * 8 + (e_q // 2) * 4 + e_x
        return pltpu.make_async_remote_copy(
            src_ref=ds.at[e], dst_ref=dr.at[e_piece], send_sem=bs.at[e], recv_sem=br.at[e_piece],
            device_id=d_peer(e), device_id_type=MESH)

    def gram(c, side):
        corner = None
        corner_parts = ()
        for row, col in QUADS:
            total = None
            for k in range(4):
                if side == 0:
                    left = xg[c, k, row * H:(row + 1) * H, :]
                    right = xg[c, k, col * H:(col + 1) * H, :]
                    dims = (((1,), (1,)), ((), ()))
                else:
                    left = xg[c, k, :, row * H:(row + 1) * H]
                    right = xg[c, k, :, col * H:(col + 1) * H]
                    dims = (((0,), (0,)), ((), ()))
                term = lax.dot_general(left, right, dims, preferred_element_type=jnp.float32)
                total = term if total is None else total + term
            if corner is None:
                corner = total[T:, T:]
                shifted = swapped(corner)
                corner_parts = (shifted, turned(shifted), turned(corner))
            for n, (i, j) in enumerate(TILES):
                if i // 2 == row and j // 2 == col:
                    i0, j0 = (i % 2) * T, (j % 2) * T
                    block = total[i0:i0 + T, j0:j0 + T]
                    if i == j:
                        block = jnp.where(low_left(), corner_parts[i], block)
                    part[c, side, :, n] = block.reshape(16, 8, T)

    def spread(c, side):
        for k in order:
            t_copy(c, side, k).start()
        xt[4 * x + 2 * c + side] = part[c, side, piece]

    order = (2, 1, 3)

    def send_x():
        for c in range(2):
            for k in order:
                x_copy(c, k).start()
            for k in order:
                x_copy(c, k).wait_send()

    @pl.when(core == 0)
    def _():
        send_x()
        pl.semaphore_signal(turn, inc=1, device_id={"dp": d, "factor": f + 1}, device_id_type=MESH)

    @pl.when(core == 1)
    def _():
        pl.semaphore_wait(turn, 1)
        send_x()

    owners = [table[f, j] for j in range(16)]
    for g in range(16):
        pick = jnp.int32(0)
        for j in range(16):
            pick = jnp.where(lax.shift_right_logical(owners[j], 4) == g, j, pick)
        items[g] = pick
    lax.fori_loop(0, 16, find_column, 0)

    def arrive(c):
        own[c].wait()
        for k in order:
            x_copy(c, k).wait_recv()

    arrive(0)
    for side in range(2):
        gram(0, side)
        z_copy(0, side, 0).start()
    for side in range(2):
        z_copy(0, side, 0).wait_recv()
        part[0, side, pl.ds(b0 * 8, 8)] += r1[side]
        z_copy(0, side, 1).start()
    arrive(1)
    for side in range(2):
        gram(1, side)
        for k in order:
            w_copy(side, k).start()
    for side in range(2):
        z_copy(0, side, 1).wait_recv()
        part[0, side, pl.ds(home, 4)] += r2[side]
        spread(0, side)
    for side in range(2):
        for k in order:
            w_copy(side, k).wait_recv()
        part[1, side, pl.ds(home, 4)] += (r3[side, 1] + r3[side, 2]) + r3[side, 3]
        spread(1, side)
    for c in range(2):
        for side in range(2):
            for k in order:
                t_copy(c, side, k).wait_recv()

    for k in range(1, 16):
        g = (f + k) % 16
        fs[g] = xt[items[g]]
        a_copy(g).start()
    fr[f] = xt[items[f]]
    for k in range(1, 16):
        a_landed((f + k) % 16).wait_recv()
    for k in range(1, 16):
        e = (d + k) % 16
        ds[e] = fr[columns[e]]
        b_copy(e).start()
    dr[piece] = fr[columns[d]]
    for k in range(1, 16):
        b_landed((d + k) % 16).wait_recv()
    out[...] = dr[...]

    for c in range(2):
        for side in range(2):
            for k in order:
                t_copy(c, side, k).wait_send()
    for side in range(2):
        for step in range(2):
            z_copy(0, side, step).wait_send()
        for k in order:
            w_copy(side, k).wait_send()
    for k in range(1, 16):
        a_copy((f + k) % 16).wait_send()
        b_copy((d + k) % 16).wait_send()


def routed(table, grads):
    tile = (NT, 8, T)
    return pl.pallas_call(
        route,
        out_shape=jax.ShapeDtypeStruct((16,) + tile, jnp.float32),
        in_specs=[
            pl.BlockSpec(memory_space=pltpu.SMEM),
            pl.BlockSpec(memory_space=pltpu.HBM),
        ],
        out_specs=pl.BlockSpec(memory_space=pltpu.VMEM),
        scratch_shapes=[
            pltpu.VMEM((2, 4, B, B), jnp.bfloat16),
            pltpu.VMEM((2, 2, 16) + tile, jnp.float32),
            pltpu.VMEM((2, 8) + tile, jnp.float32),
            pltpu.VMEM((2, 4) + tile, jnp.float32),
            pltpu.VMEM((2, 4, 4) + tile, jnp.float32),
            pltpu.VMEM((16,) + tile, jnp.float32),
            pltpu.VMEM((16,) + tile, jnp.float32),
            pltpu.VMEM((16,) + tile, jnp.float32),
            pltpu.VMEM((16,) + tile, jnp.float32),
            pltpu.VMEM((16,) + tile, jnp.float32),
            pltpu.SMEM((16,), jnp.int32),
            pltpu.SMEM((16,), jnp.int32),
            pltpu.SemaphoreType.DMA((2,)),
            pltpu.SemaphoreType.DMA((2, 4)),
            pltpu.SemaphoreType.DMA((2, 4)),
            pltpu.SemaphoreType.DMA((2, 2)),
            pltpu.SemaphoreType.DMA((2, 2)),
            pltpu.SemaphoreType.DMA((2, 4)),
            pltpu.SemaphoreType.DMA((2, 4)),
            pltpu.SemaphoreType.DMA((2, 2, 4)),
            pltpu.SemaphoreType.DMA((2, 2, 4)),
            pltpu.SemaphoreType.DMA((16,)),
            pltpu.SemaphoreType.DMA((16,)),
            pltpu.SemaphoreType.DMA((16,)),
            pltpu.SemaphoreType.DMA((16,)),
            pltpu.SemaphoreType.REGULAR,
        ],
        compiler_params=pltpu.CompilerParams(
            collective_id=0, has_side_effects=True, vmem_limit_bytes=52 * 1024 * 1024
        ),
        cost_estimate=pl.CostEstimate(flops=4 * 10**9, bytes_accessed=8 * 10**6, transcendentals=0),
        name="route",
    )(table, grads)


def split(a):
    high = a.astype(jnp.bfloat16)
    return high, (a - high.astype(jnp.float32)).astype(jnp.bfloat16)


def halves(matrix):
    return {place: split(quarter) for place, quarter in matrix.items()}


def product(a, b):
    out = {}
    for r, c in ((0, 0), (0, 1), (1, 1)):
        left, right = [], []
        for k in range(2):
            left += [a[r, k][0], a[r, k][0], a[r, k][1]]
            right += [b[k, c][0], b[k, c][1], b[k, c][0]]
        out[r, c] = jnp.dot(
            jnp.concatenate(left, axis=1), jnp.concatenate(right, axis=0), preferred_element_type=jnp.float32
        )
    out[1, 0] = out[0, 1].T
    return out


def newton(tri, old, stats, roots):
    def blend(i, j, block):
        rows, cols = slice(i * T, (i + 1) * T), slice(j * T, (j + 1) * T)
        stats[rows, cols] = BETA * old[rows, cols] + (1.0 - BETA) * block

    mask = low_left()
    kept = []
    for n, (i, j) in enumerate(TILES):
        block = tri[:, n].reshape(T, T)
        if i == j:
            kept.append(block)
            blend(i, i, jnp.where(mask, block.T, block))
        else:
            blend(i, j, block)
            blend(j, i, block.T)
    first, second, third = kept
    left = lax.broadcasted_iota(jnp.int32, (T // 2, T), 1) < T // 2
    top = jnp.where(left, first[T // 2:], turned(second[T // 2:]))
    corner = jnp.concatenate([top, turned(third[T // 2:])], axis=0)
    blend(3, 3, jnp.where(mask, corner.T, corner))

    scale = 2.5 / jnp.sqrt(jnp.sum(stats[...] * stats[...], keepdims=True) + 1e-06)
    eye = lax.broadcasted_iota(jnp.int32, (H, H), 0) == lax.broadcasted_iota(jnp.int32, (H, H), 1)

    def factor_of(matrix):
        return {
            (r, c): (jnp.where(eye, 1.25, 0.0) if r == c else 0.0) - 0.25 * quarter
            for (r, c), quarter in matrix.items()
        }

    moving = {
        (r, c): scale * stats[r * H:(r + 1) * H, c * H:(c + 1) * H] for r in range(2) for c in range(2)
    }
    root = factor_of(moving)
    factor = halves(root)
    for sweep in range(1, ITERS):
        square = halves(product(factor, factor))
        fourth = halves(product(square, square))
        moving = product(fourth, halves(moving))
        factor = halves(factor_of(moving))
        root = product(halves(root), factor)
    post = jnp.sqrt(jnp.sqrt(scale))
    for (r, c), quarter in root.items():
        roots[r * H:(r + 1) * H, c * H:(c + 1) * H] = post * quarter


def finished(tri, old):
    whole = pl.BlockSpec(memory_space=pltpu.VMEM)
    return pl.pallas_call(
        newton,
        out_shape=(jax.ShapeDtypeStruct((B, B), jnp.float32),) * 2,
        in_specs=[whole, whole],
        out_specs=(whole, whole),
        compiler_params=pltpu.CompilerParams(vmem_limit_bytes=48 * 1024 * 1024),
        cost_estimate=pl.CostEstimate(flops=13 * 10**9, bytes_accessed=4 * 10**6, transcendentals=0),
        name="newton",
    )(tri, old)


def local(gradients, old_stats, owner_table):
    tri = routed(owner_table, gradients[0])
    stats, roots = finished(tri, old_stats[0, 0])
    return (stats[None, None], roots[None, None])


def solution(mesh):
    placed = (P("dp", "factor", None, None), P("dp", "factor", None, None), P())
    return jax.shard_map(
        local,
        mesh=mesh,
        in_specs=placed,
        out_specs=(P("dp", "factor", None, None), P("dp", "factor", None, None)),
        check_vma=False,
    )
```

```python
import jax
import jax.numpy as jnp
from jax import lax
from jax.experimental import pallas as pl
from jax.experimental.pallas import tpu as pltpu
from jax.sharding import PartitionSpec as P

ITERS = 5
BETA = 0.9
B = 512
T = 128
MESH = pl.DeviceIdType.MESH
TILES = ((0, 1), (0, 2), (0, 3), (1, 2), (1, 3), (2, 3), (0, 0), (1, 1), (2, 2))
NT = len(TILES)
H = 256
QUADS = ((1, 1), (0, 0), (0, 1))


def low_left():
    rows = lax.broadcasted_iota(jnp.int32, (T, T), 0)
    cols = lax.broadcasted_iota(jnp.int32, (T, T), 1)
    return jnp.logical_and(rows >= T // 2, cols < T // 2)


def swapped(block):
    return jnp.concatenate([block[T // 2:], block[:T // 2]], axis=0)


def turned(block):
    return jnp.concatenate([block[:, T // 2:], block[:, :T // 2]], axis=1)


def route(table, grads, out, xg, part, last, r1, r2, r3, xt, fs, fr, ds, dr, items, columns,
          own_sem, xs, xr, zs, zr, ws, wr, ts, tr, as_, ar, bs, br, turn):
    d = lax.axis_index("dp")
    f = lax.axis_index("factor")
    x, zl = d // 4, d % 4
    zh, core = f // 8, f % 2
    q = zl + zh * (3 - 2 * zl)
    b0, b1 = q % 2, q // 2
    home = b0 * 8 + b1 * 4
    piece = home + x

    def dp_at(x_, q_, zh_):
        return x_ * 4 + q_ + zh_ * (3 - 2 * q_)

    def x_peer(k):
        return {"dp": dp_at((x + k) % 4, q, zh), "factor": f}

    def z_peer(step):
        flip = q + 1 - 2 * b0 if step == 0 else q + 2 - 4 * b1
        return {"dp": dp_at(x, flip, zh), "factor": f}

    def f_peer(g):
        return {"dp": dp_at(x, q, g // 8), "factor": g}

    def d_peer(e):
        return {"dp": e, "factor": f}

    barrier = pltpu.get_barrier_semaphore()
    for k in range(1, 16):
        pl.semaphore_signal(barrier, inc=1, device_id=d_peer((d + k) % 16), device_id_type=MESH)
        pl.semaphore_signal(barrier, inc=1, device_id=f_peer((f + k) % 16), device_id_type=MESH)
    own = [pltpu.make_async_copy(grads.at[2 * x + c], xg.at[c, 0], own_sem.at[c]) for c in range(2)]
    for copy in own:
        copy.start()

    def find_column(e, carry):
        def scan(c, found):
            for j in range(16):
                found = jnp.where(table[c, j] == f * 16 + e, c, found)
            return found
        columns[e] = lax.fori_loop(0, 16, scan, jnp.int32(0))
        return carry

    pl.semaphore_wait(barrier, 30)

    def x_copy(c, k):
        return pltpu.make_async_remote_copy(
            src_ref=grads.at[2 * ((x + k) % 4) + c], dst_ref=xg.at[c, k],
            send_sem=xs.at[c, k], recv_sem=xr.at[c, k], device_id=x_peer(k), device_id_type=MESH)

    def z_copy(side, step):
        if step == 0:
            src, dst = part.at[side, pl.ds((1 - b0) * 8, 8)], r1.at[side]
        else:
            src, dst = part.at[side, pl.ds(b0 * 8 + (1 - b1) * 4, 4)], r2.at[side]
        return pltpu.make_async_remote_copy(
            src_ref=src, dst_ref=dst, send_sem=zs.at[side, step], recv_sem=zr.at[side, step],
            device_id=z_peer(step), device_id_type=MESH)

    def t_copy(side, k):
        return pltpu.make_async_remote_copy(
            src_ref=part.at[side, home + (x + k) % 4], dst_ref=xt.at[4 * x + side],
            send_sem=ts.at[side, k], recv_sem=tr.at[side, k], device_id=x_peer(k), device_id_type=MESH)

    def piece_of(e):
        e_x, e_zl = e // 4, e % 4
        e_q = e_zl + zh * (3 - 2 * e_zl)
        return (e_q % 2) * 8 + (e_q // 2) * 4 + e_x

    def w_copy(e):
        return pltpu.make_async_remote_copy(
            src_ref=last.at[piece_of(e)], dst_ref=r3.at[d], send_sem=ws.at[e], recv_sem=wr.at[d],
            device_id=d_peer(e), device_id_type=MESH)

    def w_landed(e):
        return pltpu.make_async_remote_copy(
            src_ref=last.at[piece_of(e)], dst_ref=r3.at[e], send_sem=ws.at[e], recv_sem=wr.at[e],
            device_id=d_peer(e), device_id_type=MESH)

    def a_copy(g):
        return pltpu.make_async_remote_copy(
            src_ref=fs.at[g], dst_ref=fr.at[f], send_sem=as_.at[g], recv_sem=ar.at[f],
            device_id=f_peer(g), device_id_type=MESH)

    def a_landed(g):
        return pltpu.make_async_remote_copy(
            src_ref=fs.at[g], dst_ref=fr.at[g], send_sem=as_.at[g], recv_sem=ar.at[g],
            device_id=f_peer(g), device_id_type=MESH)

    def b_copy(e):
        return pltpu.make_async_remote_copy(
            src_ref=ds.at[e], dst_ref=dr.at[piece], send_sem=bs.at[e], recv_sem=br.at[piece],
            device_id=d_peer(e), device_id_type=MESH)

    def b_landed(e):
        e_piece = piece_of(e)
        return pltpu.make_async_remote_copy(
            src_ref=ds.at[e], dst_ref=dr.at[e_piece], send_sem=bs.at[e], recv_sem=br.at[e_piece],
            device_id=d_peer(e), device_id_type=MESH)

    def gram(c, side):
        corner = None
        corner_parts = ()
        for row, col in QUADS:
            total = None
            for k in range(4):
                if side == 0:
                    left = xg[c, k, row * H:(row + 1) * H, :]
                    right = xg[c, k, col * H:(col + 1) * H, :]
                    dims = (((1,), (1,)), ((), ()))
                else:
                    left = xg[c, k, :, row * H:(row + 1) * H]
                    right = xg[c, k, :, col * H:(col + 1) * H]
                    dims = (((0,), (0,)), ((), ()))
                term = lax.dot_general(left, right, dims, preferred_element_type=jnp.float32)
                total = term if total is None else total + term
            if corner is None:
                corner = total[T:, T:]
                shifted = swapped(corner)
                corner_parts = (shifted, turned(shifted), turned(corner))
            for n, (i, j) in enumerate(TILES):
                if i // 2 == row and j // 2 == col:
                    i0, j0 = (i % 2) * T, (j % 2) * T
                    block = total[i0:i0 + T, j0:j0 + T]
                    if i == j:
                        block = jnp.where(low_left(), corner_parts[i], block)
                    if c == 0:
                        part[side, :, n] = block.reshape(16, 8, T)
                    else:
                        last[:, side, n] = block.reshape(16, 8, T)

    order = (2, 1, 3)
    partner = {"dp": d, "factor": f + 1 - 2 * core}

    def send_x(c):
        for k in order:
            x_copy(c, k).start()

    def sent_x(c):
        for k in order:
            x_copy(c, k).wait_send()

    def arrive(c):
        own[c].wait()
        for k in order:
            x_copy(c, k).wait_recv()

    @pl.when(core == 1)
    def _():
        pl.semaphore_wait(turn, 1)

    send_x(0)
    for g in range(16):
        pick = jnp.int32(0)
        for j in range(16):
            pick = jnp.where(lax.shift_right_logical(table[f, j], 4) == g, j, pick)
        items[g] = pick
    lax.fori_loop(0, 16, find_column, 0)
    sent_x(0)
    pl.semaphore_signal(turn, inc=1, device_id=partner, device_id_type=MESH)

    arrive(0)
    for side in range(2):
        gram(0, side)
        z_copy(side, 0).start()
    for side in range(2):
        z_copy(side, 0).wait_recv()
        part[side, pl.ds(b0 * 8, 8)] += r1[side]
        z_copy(side, 1).start()
    pl.semaphore_wait(turn, 1)
    send_x(1)
    for side in range(2):
        z_copy(side, 1).wait_recv()
        part[side, pl.ds(home, 4)] += r2[side]
        for k in order:
            t_copy(side, k).start()
        xt[4 * x + side] = part[side, piece]
    sent_x(1)

    @pl.when(core == 0)
    def _():
        pl.semaphore_signal(turn, inc=1, device_id=partner, device_id_type=MESH)

    arrive(1)
    for side in range(2):
        gram(1, side)
    for k in range(1, 16):
        w_copy((d + k) % 16).start()
    r3[d] = last[piece]
    for side in range(2):
        for k in order:
            t_copy(side, k).wait_recv()
    for k in range(1, 16):
        w_landed((d + k) % 16).wait_recv()
    for i in range(4):
        xt[4 * i + 2:4 * i + 4] = (r3[4 * i] + r3[4 * i + 1]) + (r3[4 * i + 2] + r3[4 * i + 3])

    for k in range(1, 16):
        g = (f + k) % 16
        fs[g] = xt[items[g]]
        a_copy(g).start()
    fr[f] = xt[items[f]]
    for k in range(1, 16):
        a_landed((f + k) % 16).wait_recv()
    for k in range(1, 16):
        e = (d + k) % 16
        ds[e] = fr[columns[e]]
        b_copy(e).start()
    dr[piece] = fr[columns[d]]
    for k in range(1, 16):
        b_landed((d + k) % 16).wait_recv()
    out[...] = dr[...]

    for side in range(2):
        for step in range(2):
            z_copy(side, step).wait_send()
        for k in order:
            t_copy(side, k).wait_send()
    for k in range(1, 16):
        w_copy((d + k) % 16).wait_send()
    for k in range(1, 16):
        a_copy((f + k) % 16).wait_send()
        b_copy((d + k) % 16).wait_send()


def routed(table, grads):
    tile = (NT, 8, T)
    return pl.pallas_call(
        route,
        out_shape=jax.ShapeDtypeStruct((16,) + tile, jnp.float32),
        in_specs=[
            pl.BlockSpec(memory_space=pltpu.SMEM),
            pl.BlockSpec(memory_space=pltpu.HBM),
        ],
        out_specs=pl.BlockSpec(memory_space=pltpu.VMEM),
        scratch_shapes=[
            pltpu.VMEM((2, 4, B, B), jnp.bfloat16),
            pltpu.VMEM((2, 16) + tile, jnp.float32),
            pltpu.VMEM((16, 2) + tile, jnp.float32),
            pltpu.VMEM((2, 8) + tile, jnp.float32),
            pltpu.VMEM((2, 4) + tile, jnp.float32),
            pltpu.VMEM((16, 2) + tile, jnp.float32),
            pltpu.VMEM((16,) + tile, jnp.float32),
            pltpu.VMEM((16,) + tile, jnp.float32),
            pltpu.VMEM((16,) + tile, jnp.float32),
            pltpu.VMEM((16,) + tile, jnp.float32),
            pltpu.VMEM((16,) + tile, jnp.float32),
            pltpu.SMEM((16,), jnp.int32),
            pltpu.SMEM((16,), jnp.int32),
            pltpu.SemaphoreType.DMA((2,)),
            pltpu.SemaphoreType.DMA((2, 4)),
            pltpu.SemaphoreType.DMA((2, 4)),
            pltpu.SemaphoreType.DMA((2, 2)),
            pltpu.SemaphoreType.DMA((2, 2)),
            pltpu.SemaphoreType.DMA((16,)),
            pltpu.SemaphoreType.DMA((16,)),
            pltpu.SemaphoreType.DMA((2, 4)),
            pltpu.SemaphoreType.DMA((2, 4)),
            pltpu.SemaphoreType.DMA((16,)),
            pltpu.SemaphoreType.DMA((16,)),
            pltpu.SemaphoreType.DMA((16,)),
            pltpu.SemaphoreType.DMA((16,)),
            pltpu.SemaphoreType.REGULAR,
        ],
        compiler_params=pltpu.CompilerParams(
            collective_id=0, has_side_effects=True, vmem_limit_bytes=52 * 1024 * 1024
        ),
        cost_estimate=pl.CostEstimate(flops=4 * 10**9, bytes_accessed=8 * 10**6, transcendentals=0),
        name="route",
    )(table, grads)


def split(a):
    high = a.astype(jnp.bfloat16)
    return high, (a - high.astype(jnp.float32)).astype(jnp.bfloat16)


def halves(matrix):
    return {place: split(quarter) for place, quarter in matrix.items()}


def product(a, b):
    out = {}
    for r, c in ((0, 0), (0, 1), (1, 1)):
        left, right = [], []
        for k in range(2):
            left += [a[r, k][0], a[r, k][0], a[r, k][1]]
            right += [b[k, c][0], b[k, c][1], b[k, c][0]]
        out[r, c] = jnp.dot(
            jnp.concatenate(left, axis=1), jnp.concatenate(right, axis=0), preferred_element_type=jnp.float32
        )
    out[1, 0] = out[0, 1].T
    return out


def newton(tri, old, stats, roots):
    def blend(i, j, block):
        rows, cols = slice(i * T, (i + 1) * T), slice(j * T, (j + 1) * T)
        stats[rows, cols] = BETA * old[rows, cols] + (1.0 - BETA) * block

    mask = low_left()
    kept = []
    for n, (i, j) in enumerate(TILES):
        block = tri[:, n].reshape(T, T)
        if i == j:
            kept.append(block)
            blend(i, i, jnp.where(mask, block.T, block))
        else:
            blend(i, j, block)
            blend(j, i, block.T)
    first, second, third = kept
    left = lax.broadcasted_iota(jnp.int32, (T // 2, T), 1) < T // 2
    top = jnp.where(left, first[T // 2:], turned(second[T // 2:]))
    corner = jnp.concatenate([top, turned(third[T // 2:])], axis=0)
    blend(3, 3, jnp.where(mask, corner.T, corner))

    scale = 2.5 / jnp.sqrt(jnp.sum(stats[...] * stats[...], keepdims=True) + 1e-06)
    eye = lax.broadcasted_iota(jnp.int32, (H, H), 0) == lax.broadcasted_iota(jnp.int32, (H, H), 1)

    def factor_of(matrix):
        return {
            (r, c): (jnp.where(eye, 1.25, 0.0) if r == c else 0.0) - 0.25 * quarter
            for (r, c), quarter in matrix.items()
        }

    moving = {
        (r, c): scale * stats[r * H:(r + 1) * H, c * H:(c + 1) * H] for r in range(2) for c in range(2)
    }
    root = factor_of(moving)
    factor = halves(root)
    for sweep in range(1, ITERS):
        square = halves(product(factor, factor))
        fourth = halves(product(square, square))
        moving = product(fourth, halves(moving))
        factor = halves(factor_of(moving))
        root = product(halves(root), factor)
    post = jnp.sqrt(jnp.sqrt(scale))
    for (r, c), quarter in root.items():
        roots[r * H:(r + 1) * H, c * H:(c + 1) * H] = post * quarter


def finished(tri, old):
    whole = pl.BlockSpec(memory_space=pltpu.VMEM)
    return pl.pallas_call(
        newton,
        out_shape=(jax.ShapeDtypeStruct((B, B), jnp.float32),) * 2,
        in_specs=[whole, whole],
        out_specs=(whole, whole),
        compiler_params=pltpu.CompilerParams(vmem_limit_bytes=48 * 1024 * 1024),
        cost_estimate=pl.CostEstimate(flops=13 * 10**9, bytes_accessed=4 * 10**6, transcendentals=0),
        name="newton",
    )(tri, old)


def local(gradients, old_stats, owner_table):
    tri = routed(owner_table, gradients[0])
    stats, roots = finished(tri, old_stats[0, 0])
    return (stats[None, None], roots[None, None])


def solution(mesh):
    placed = (P("dp", "factor", None, None), P("dp", "factor", None, None), P())
    return jax.shard_map(
        local,
        mesh=mesh,
        in_specs=placed,
        out_specs=(P("dp", "factor", None, None), P("dp", "factor", None, None)),
        check_vma=False,
    )
```

```python
import jax
import jax.numpy as jnp
from jax import lax
from jax.experimental import pallas as pl
from jax.experimental.pallas import tpu as pltpu
from jax.sharding import PartitionSpec as P

ITERS = 5
BETA = 0.9
B = 512
T = 128
MESH = pl.DeviceIdType.MESH
PARTS = (((0, 2), (0, 3), (1, 2), (1, 3)), ((0, 1), (2, 3), (0, 0), (1, 1), (2, 2)))
QUADS = (((0, 1),), ((1, 1), (0, 0)))
H = 256


def low_left():
    rows = lax.broadcasted_iota(jnp.int32, (T, T), 0)
    cols = lax.broadcasted_iota(jnp.int32, (T, T), 1)
    return jnp.logical_and(rows >= T // 2, cols < T // 2)


def swapped(block):
    return jnp.concatenate([block[T // 2:], block[:T // 2]], axis=0)


def turned(block):
    return jnp.concatenate([block[:, T // 2:], block[:, :T // 2]], axis=1)


def route(table, grads, out0, out1, xg, part0, part1, last0, last1, r10, r11, r20, r21, r30, r31, xt0, xt1, fs0, fs1, fr0, fr1,
          ds0, ds1, dr0, dr1, items, columns, own_sem, xs, xr, zs, zr, ws, wr, ts, tr, as_, ar, bs, br, turn):
    r1, r2 = (r10, r11), (r20, r21)
    part, last, r3, xt = (part0, part1), (last0, last1), (r30, r31), (xt0, xt1)
    fs, fr, ds, dr, out = (fs0, fs1), (fr0, fr1), (ds0, ds1), (dr0, dr1), (out0, out1)
    d = lax.axis_index("dp")
    f = lax.axis_index("factor")
    x, zl = d // 4, d % 4
    zh, core = f // 8, f % 2
    q = zl + zh * (3 - 2 * zl)
    b0, b1 = q % 2, q // 2
    home = b0 * 8 + b1 * 4
    piece = home + x

    def dp_at(x_, q_, zh_):
        return x_ * 4 + q_ + zh_ * (3 - 2 * q_)

    def x_peer(k):
        return {"dp": dp_at((x + k) % 4, q, zh), "factor": f}

    def z_peer(step):
        flip = q + 1 - 2 * b0 if step == 0 else q + 2 - 4 * b1
        return {"dp": dp_at(x, flip, zh), "factor": f}

    def f_peer(g):
        return {"dp": dp_at(x, q, g // 8), "factor": g}

    def d_peer(e):
        return {"dp": e, "factor": f}

    barrier = pltpu.get_barrier_semaphore()
    for k in range(1, 16):
        pl.semaphore_signal(barrier, inc=1, device_id=d_peer((d + k) % 16), device_id_type=MESH)
        pl.semaphore_signal(barrier, inc=1, device_id=f_peer((f + k) % 16), device_id_type=MESH)
    own = [pltpu.make_async_copy(grads.at[2 * x + c], xg.at[c, 0], own_sem.at[c]) for c in range(2)]
    for copy in own:
        copy.start()

    def find_column(e, carry):
        def scan(c, found):
            for j in range(16):
                found = jnp.where(table[c, j] == f * 16 + e, c, found)
            return found
        columns[e] = lax.fori_loop(0, 16, scan, jnp.int32(0))
        return carry

    pl.semaphore_wait(barrier, 30)

    def x_copy(c, k):
        return pltpu.make_async_remote_copy(
            src_ref=grads.at[2 * ((x + k) % 4) + c], dst_ref=xg.at[c, k],
            send_sem=xs.at[c, k], recv_sem=xr.at[c, k], device_id=x_peer(k), device_id_type=MESH)

    def z_copy(h, step):
        if step == 0:
            src, dst = part[h].at[pl.ds((1 - b0) * 8, 8)], r1[h]
        else:
            src, dst = part[h].at[pl.ds(b0 * 8 + (1 - b1) * 4, 4)], r2[h]
        return pltpu.make_async_remote_copy(
            src_ref=src, dst_ref=dst, send_sem=zs.at[h, step], recv_sem=zr.at[h, step],
            device_id=z_peer(step), device_id_type=MESH)

    def t_copy(h, k):
        return pltpu.make_async_remote_copy(
            src_ref=part[h].at[home + (x + k) % 4], dst_ref=xt[h].at[pl.ds(4 * x, 2)],
            send_sem=ts.at[h, k], recv_sem=tr.at[h, k], device_id=x_peer(k), device_id_type=MESH)

    def piece_of(e):
        e_x, e_zl = e // 4, e % 4
        e_q = e_zl + zh * (3 - 2 * e_zl)
        return (e_q % 2) * 8 + (e_q // 2) * 4 + e_x

    def w_copy(h, e):
        return pltpu.make_async_remote_copy(
            src_ref=last[h].at[piece_of(e)], dst_ref=r3[h].at[d], send_sem=ws.at[h, e], recv_sem=wr.at[h, d],
            device_id=d_peer(e), device_id_type=MESH)

    def w_landed(h, e):
        return pltpu.make_async_remote_copy(
            src_ref=last[h].at[piece_of(e)], dst_ref=r3[h].at[e], send_sem=ws.at[h, e], recv_sem=wr.at[h, e],
            device_id=d_peer(e), device_id_type=MESH)

    def a_copy(h, g):
        return pltpu.make_async_remote_copy(
            src_ref=fs[h].at[g], dst_ref=fr[h].at[f], send_sem=as_.at[h, g], recv_sem=ar.at[h, f],
            device_id=f_peer(g), device_id_type=MESH)

    def a_landed(h, g):
        return pltpu.make_async_remote_copy(
            src_ref=fs[h].at[g], dst_ref=fr[h].at[g], send_sem=as_.at[h, g], recv_sem=ar.at[h, g],
            device_id=f_peer(g), device_id_type=MESH)

    def b_copy(h, e):
        return pltpu.make_async_remote_copy(
            src_ref=ds[h].at[e], dst_ref=dr[h].at[piece], send_sem=bs.at[h, e], recv_sem=br.at[h, piece],
            device_id=d_peer(e), device_id_type=MESH)

    def b_landed(h, e):
        e_piece = piece_of(e)
        return pltpu.make_async_remote_copy(
            src_ref=ds[h].at[e], dst_ref=dr[h].at[e_piece], send_sem=bs.at[h, e], recv_sem=br.at[h, e_piece],
            device_id=d_peer(e), device_id_type=MESH)

    def gram(c, h, side):
        corner = None
        for row, col in QUADS[h]:
            total = None
            for k in range(4):
                if side == 0:
                    left = xg[c, k, row * H:(row + 1) * H, :]
                    right = xg[c, k, col * H:(col + 1) * H, :]
                    dims = (((1,), (1,)), ((), ()))
                else:
                    left = xg[c, k, :, row * H:(row + 1) * H]
                    right = xg[c, k, :, col * H:(col + 1) * H]
                    dims = (((0,), (0,)), ((), ()))
                term = lax.dot_general(left, right, dims, preferred_element_type=jnp.float32)
                total = term if total is None else total + term
            if (row, col) == (1, 1):
                corner = total[T:, T:]
                shifted = swapped(corner)
                corner_parts = (shifted, turned(shifted), turned(corner))
            for n, (i, j) in enumerate(PARTS[h]):
                if i // 2 == row and j // 2 == col:
                    i0, j0 = (i % 2) * T, (j % 2) * T
                    block = total[i0:i0 + T, j0:j0 + T]
                    if i == j:
                        block = jnp.where(low_left(), corner_parts[i], block)
                    kept = part if c == 0 else last
                    kept[h][:, side, n] = block.reshape(16, 8, T)

    order = (2, 1, 3)
    partner = {"dp": d, "factor": f + 1 - 2 * core}

    def send_x(c):
        for k in order:
            x_copy(c, k).start()

    def arrive(c):
        own[c].wait()
        for k in order:
            x_copy(c, k).wait_recv()

    @pl.when(core == 1)
    def _():
        pl.semaphore_wait(turn, 1)

    send_x(0)
    for g in range(16):
        pick = jnp.int32(0)
        for j in range(16):
            pick = jnp.where(lax.shift_right_logical(table[f, j], 4) == g, j, pick)
        items[g] = pick
    lax.fori_loop(0, 16, find_column, 0)
    x_copy(0, 1).wait_send()
    pl.semaphore_signal(turn, inc=1, device_id=partner, device_id_type=MESH)

    arrive(0)
    for h in range(2):
        for side in range(2):
            gram(0, h, side)
        z_copy(h, 0).start()
    for h in range(2):
        z_copy(h, 0).wait_recv()
        part[h][pl.ds(b0 * 8, 8)] += r1[h][...]
        z_copy(h, 1).start()
    pl.semaphore_wait(turn, 1)
    send_x(1)
    for h in range(2):
        z_copy(h, 1).wait_recv()
        part[h][pl.ds(home, 4)] += r2[h][...]
        for k in order:
            t_copy(h, k).start()
        xt[h][pl.ds(4 * x, 2)] = part[h][piece]
    x_copy(1, 1).wait_send()

    @pl.when(core == 0)
    def _():
        pl.semaphore_signal(turn, inc=1, device_id=partner, device_id_type=MESH)

    arrive(1)
    for h in range(2):
        for side in range(2):
            gram(1, h, side)
        for k in range(1, 16):
            w_copy(h, (d + k) % 16).start()
        r3[h][d] = last[h][piece]
    for h in range(2):
        for k in order:
            t_copy(h, k).wait_recv()
    for h in range(2):
        for k in range(1, 16):
            w_landed(h, (d + k) % 16).wait_recv()
        for i in range(4):
            here = r3[h][4 * i:4 * i + 4]
            xt[h][4 * i + 2:4 * i + 4] = (here[0] + here[1]) + (here[2] + here[3])
        for k in range(1, 16):
            g = (f + k) % 16
            fs[h][g] = xt[h][items[g]]
            a_copy(h, g).start()
        fr[h][f] = xt[h][items[f]]
    for h in range(2):
        for k in range(1, 16):
            a_landed(h, (f + k) % 16).wait_recv()
        for k in range(1, 16):
            e = (d + k) % 16
            ds[h][e] = fr[h][columns[e]]
            b_copy(h, e).start()
        dr[h][piece] = fr[h][columns[d]]
    for h in range(2):
        for k in range(1, 16):
            b_landed(h, (d + k) % 16).wait_recv()
        out[h][...] = dr[h][...]

    for c in range(2):
        for k in (2, 3):
            x_copy(c, k).wait_send()
    for h in range(2):
        for step in range(2):
            z_copy(h, step).wait_send()
        for k in order:
            t_copy(h, k).wait_send()
        for k in range(1, 16):
            w_copy(h, (d + k) % 16).wait_send()
            a_copy(h, (f + k) % 16).wait_send()
            b_copy(h, (d + k) % 16).wait_send()


def routed(table, grads):
    tiles = [(len(blocks), 8, T) for blocks in PARTS]

    def buffers(*lead):
        return [pltpu.VMEM(lead + tile, jnp.float32) for tile in tiles]

    def semaphores(*shape):
        return [pltpu.SemaphoreType.DMA(shape)] * 2

    return pl.pallas_call(
        route,
        out_shape=tuple(jax.ShapeDtypeStruct((16,) + tile, jnp.float32) for tile in tiles),
        in_specs=[
            pl.BlockSpec(memory_space=pltpu.SMEM),
            pl.BlockSpec(memory_space=pltpu.HBM),
        ],
        out_specs=(pl.BlockSpec(memory_space=pltpu.VMEM),) * 2,
        scratch_shapes=[
            pltpu.VMEM((2, 4, B, B), jnp.bfloat16),
            *buffers(16, 2),
            *buffers(16, 2),
            *buffers(8, 2),
            *buffers(4, 2),
            *buffers(16, 2),
            *buffers(16),
            *buffers(16),
            *buffers(16),
            *buffers(16),
            *buffers(16),
            pltpu.SMEM((16,), jnp.int32),
            pltpu.SMEM((16,), jnp.int32),
            pltpu.SemaphoreType.DMA((2,)),
            *semaphores(2, 4),
            *semaphores(2, 2),
            *semaphores(2, 16),
            *semaphores(2, 4),
            *semaphores(2, 16),
            *semaphores(2, 16),
            pltpu.SemaphoreType.REGULAR,
        ],
        compiler_params=pltpu.CompilerParams(
            collective_id=0, has_side_effects=True, vmem_limit_bytes=52 * 1024 * 1024
        ),
        cost_estimate=pl.CostEstimate(flops=4 * 10**9, bytes_accessed=8 * 10**6, transcendentals=0),
        name="route",
    )(table, grads)


def split(a):
    high = a.astype(jnp.bfloat16)
    return high, (a - high.astype(jnp.float32)).astype(jnp.bfloat16)


def halves(matrix):
    return {place: split(quarter) for place, quarter in matrix.items()}


def product(a, b):
    out = {}
    for r, c in ((0, 0), (0, 1), (1, 1)):
        left, right = [], []
        for k in range(2):
            left += [a[r, k][0], a[r, k][0], a[r, k][1]]
            right += [b[k, c][0], b[k, c][1], b[k, c][0]]
        out[r, c] = jnp.dot(
            jnp.concatenate(left, axis=1), jnp.concatenate(right, axis=0), preferred_element_type=jnp.float32
        )
    out[1, 0] = out[0, 1].T
    return out


def newton(tri0, tri1, old, stats, roots):
    def blend(i, j, block):
        rows, cols = slice(i * T, (i + 1) * T), slice(j * T, (j + 1) * T)
        stats[rows, cols] = BETA * old[rows, cols] + (1.0 - BETA) * block

    mask = low_left()
    kept = []
    for tri, n, (i, j) in [(tri, n, p) for tri, ps in zip((tri0, tri1), PARTS) for n, p in enumerate(ps)]:
        block = tri[:, n].reshape(T, T)
        if i == j:
            kept.append(block)
            blend(i, i, jnp.where(mask, block.T, block))
        else:
            blend(i, j, block)
            blend(j, i, block.T)
    first, second, third = kept
    left = lax.broadcasted_iota(jnp.int32, (T // 2, T), 1) < T // 2
    top = jnp.where(left, first[T // 2:], turned(second[T // 2:]))
    corner = jnp.concatenate([top, turned(third[T // 2:])], axis=0)
    blend(3, 3, jnp.where(mask, corner.T, corner))

    scale = 2.5 / jnp.sqrt(jnp.sum(stats[...] * stats[...], keepdims=True) + 1e-06)
    eye = lax.broadcasted_iota(jnp.int32, (H, H), 0) == lax.broadcasted_iota(jnp.int32, (H, H), 1)

    def factor_of(matrix):
        return {
            (r, c): (jnp.where(eye, 1.25, 0.0) if r == c else 0.0) - 0.25 * quarter
            for (r, c), quarter in matrix.items()
        }

    moving = {
        (r, c): scale * stats[r * H:(r + 1) * H, c * H:(c + 1) * H] for r in range(2) for c in range(2)
    }
    root = factor_of(moving)
    factor = halves(root)
    for sweep in range(1, ITERS):
        square = halves(product(factor, factor))
        fourth = halves(product(square, square))
        moving = product(fourth, halves(moving))
        factor = halves(factor_of(moving))
        root = product(halves(root), factor)
    post = jnp.sqrt(jnp.sqrt(scale))
    for (r, c), quarter in root.items():
        roots[r * H:(r + 1) * H, c * H:(c + 1) * H] = post * quarter


def finished(tri0, tri1, old):
    whole = pl.BlockSpec(memory_space=pltpu.VMEM)
    return pl.pallas_call(
        newton,
        out_shape=(jax.ShapeDtypeStruct((B, B), jnp.float32),) * 2,
        in_specs=[whole] * 3,
        out_specs=(whole, whole),
        compiler_params=pltpu.CompilerParams(vmem_limit_bytes=48 * 1024 * 1024),
        cost_estimate=pl.CostEstimate(flops=13 * 10**9, bytes_accessed=4 * 10**6, transcendentals=0),
        name="newton",
    )(tri0, tri1, old)


def local(gradients, old_stats, owner_table):
    tri0, tri1 = routed(owner_table, gradients[0])
    stats, roots = finished(tri0, tri1, old_stats[0, 0])
    return (stats[None, None], roots[None, None])


def solution(mesh):
    placed = (P("dp", "factor", None, None), P("dp", "factor", None, None), P())
    return jax.shard_map(
        local,
        mesh=mesh,
        in_specs=placed,
        out_specs=(P("dp", "factor", None, None), P("dp", "factor", None, None)),
        check_vma=False,
    )
```

```python
import jax
import jax.numpy as jnp
from jax import lax
from jax.experimental import pallas as pl
from jax.experimental.pallas import tpu as pltpu
from jax.sharding import PartitionSpec as P

ITERS = 5
BETA = 0.9
B = 512
T = 128
MESH = pl.DeviceIdType.MESH
PARTS = (((0, 2), (0, 3), (1, 2), (1, 3)), ((0, 1), (2, 3), (0, 0), (1, 1), (2, 2)))
QUADS = (((0, 1),), ((1, 1), (0, 0)))
H = 256


def low_left():
    rows = lax.broadcasted_iota(jnp.int32, (T, T), 0)
    cols = lax.broadcasted_iota(jnp.int32, (T, T), 1)
    return jnp.logical_and(rows >= T // 2, cols < T // 2)


def swapped(block):
    return jnp.concatenate([block[T // 2:], block[:T // 2]], axis=0)


def turned(block):
    return jnp.concatenate([block[:, T // 2:], block[:, :T // 2]], axis=1)


def route(table, grads, out0, out1, xg, part0, part1, last0, last1, r10, r11, r20, r21, r30, r31, xt0, xt1, fs0, fs1, fr0, fr1,
          ds0, ds1, dr0, dr1, items, columns, own_sem, xs, xr, zs, zr, ws, wr, ts, tr, as_, ar, bs, br, turn, ready):
    r1, r2 = (r10, r11), (r20, r21)
    part, last, r3, xt = (part0, part1), (last0, last1), (r30, r31), (xt0, xt1)
    fs, fr, ds, dr, out = (fs0, fs1), (fr0, fr1), (ds0, ds1), (dr0, dr1), (out0, out1)
    d = lax.axis_index("dp")
    f = lax.axis_index("factor")
    x, zl = d // 4, d % 4
    zh, y, core = f // 8, (f // 2) % 4, f % 2
    q = zl + zh * (3 - 2 * zl)
    b0, b1 = q % 2, q // 2
    home = b0 * 8 + b1 * 4
    piece = home + x

    def dp_at(x_, q_, zh_):
        return x_ * 4 + q_ + zh_ * (3 - 2 * q_)

    def x_peer(k):
        return {"dp": dp_at((x + k) % 4, q, zh), "factor": f}

    def z_peer(step):
        flip = q + 1 - 2 * b0 if step == 0 else q + 2 - 4 * b1
        return {"dp": dp_at(x, flip, zh), "factor": f}

    def f_peer(g):
        return {"dp": dp_at(x, q, g // 8), "factor": g}

    def d_peer(e):
        return {"dp": e, "factor": f}

    partner = {"dp": d, "factor": f + 1 - 2 * core}
    along_z = [{"dp": dp_at(x, (q + k) % 4, zh), "factor": f} for k in range(1, 4)]
    along_y = [{"dp": d, "factor": zh * 8 + ((y + k) % 4) * 2 + core} for k in range(1, 4)]
    across = {"dp": dp_at(x, q, 1 - zh), "factor": (1 - zh) * 8 + y * 2 + core}
    barrier = pltpu.get_barrier_semaphore()
    for peer in [x_peer(k) for k in range(1, 4)] + [partner] + along_z + along_y + [across]:
        pl.semaphore_signal(barrier, inc=1, device_id=peer, device_id_type=MESH)
    own = [pltpu.make_async_copy(grads.at[2 * x + c], xg.at[c, 0], own_sem.at[c]) for c in range(2)]
    for copy in own:
        copy.start()

    others_d = [dp_at((x + k // 2) % 4, (1 - b1) * 2 + k % 2, zh) for k in range(8)]
    others_d += [dp_at((x + k // 2) % 4, b1 * 2 + (b0 + k) % 2, zh) for k in range(1, 8)]
    others_f = [(1 - zh) * 8 + (f + k) % 8 for k in range(8)] + [zh * 8 + (f + k) % 8 for k in range(1, 8)]

    def find_column(e, carry):
        def scan(c, found):
            for j in range(16):
                found = jnp.where(table[c, j] == f * 16 + e, c, found)
            return found
        columns[e] = lax.fori_loop(0, 16, scan, jnp.int32(0))
        return carry

    pl.semaphore_wait(barrier, 11)

    def x_copy(c, k):
        return pltpu.make_async_remote_copy(
            src_ref=grads.at[2 * ((x + k) % 4) + c], dst_ref=xg.at[c, k],
            send_sem=xs.at[c, k], recv_sem=xr.at[c, k], device_id=x_peer(k), device_id_type=MESH)

    def z_copy(h, step):
        if step == 0:
            src, dst = part[h].at[pl.ds((1 - b0) * 8, 8)], r1[h]
        else:
            src, dst = part[h].at[pl.ds(b0 * 8 + (1 - b1) * 4, 4)], r2[h]
        return pltpu.make_async_remote_copy(
            src_ref=src, dst_ref=dst, send_sem=zs.at[h, step], recv_sem=zr.at[h, step],
            device_id=z_peer(step), device_id_type=MESH)

    def t_copy(h, k):
        return pltpu.make_async_remote_copy(
            src_ref=part[h].at[home + (x + k) % 4], dst_ref=xt[h].at[pl.ds(4 * x, 2)],
            send_sem=ts.at[h, k], recv_sem=tr.at[h, k], device_id=x_peer(k), device_id_type=MESH)

    def piece_of(e):
        e_x, e_zl = e // 4, e % 4
        e_q = e_zl + zh * (3 - 2 * e_zl)
        return (e_q % 2) * 8 + (e_q // 2) * 4 + e_x

    def w_copy(h, e):
        return pltpu.make_async_remote_copy(
            src_ref=last[h].at[piece_of(e)], dst_ref=r3[h].at[d], send_sem=ws.at[h, e], recv_sem=wr.at[h, d],
            device_id=d_peer(e), device_id_type=MESH)

    def w_landed(h, e):
        return pltpu.make_async_remote_copy(
            src_ref=last[h].at[piece_of(e)], dst_ref=r3[h].at[e], send_sem=ws.at[h, e], recv_sem=wr.at[h, e],
            device_id=d_peer(e), device_id_type=MESH)

    def a_copy(h, g):
        return pltpu.make_async_remote_copy(
            src_ref=fs[h].at[g], dst_ref=fr[h].at[f], send_sem=as_.at[h, g], recv_sem=ar.at[h, f],
            device_id=f_peer(g), device_id_type=MESH)

    def a_landed(h, g):
        return pltpu.make_async_remote_copy(
            src_ref=fs[h].at[g], dst_ref=fr[h].at[g], send_sem=as_.at[h, g], recv_sem=ar.at[h, g],
            device_id=f_peer(g), device_id_type=MESH)

    def b_copy(h, e):
        return pltpu.make_async_remote_copy(
            src_ref=ds[h].at[e], dst_ref=dr[h].at[piece], send_sem=bs.at[h, e], recv_sem=br.at[h, piece],
            device_id=d_peer(e), device_id_type=MESH)

    def b_landed(h, e):
        e_piece = piece_of(e)
        return pltpu.make_async_remote_copy(
            src_ref=ds[h].at[e], dst_ref=dr[h].at[e_piece], send_sem=bs.at[h, e], recv_sem=br.at[h, e_piece],
            device_id=d_peer(e), device_id_type=MESH)

    def gram(c, h, side):
        corner = None
        for row, col in QUADS[h]:
            total = None
            for k in range(4):
                if side == 0:
                    left = xg[c, k, row * H:(row + 1) * H, :]
                    right = xg[c, k, col * H:(col + 1) * H, :]
                    dims = (((1,), (1,)), ((), ()))
                else:
                    left = xg[c, k, :, row * H:(row + 1) * H]
                    right = xg[c, k, :, col * H:(col + 1) * H]
                    dims = (((0,), (0,)), ((), ()))
                term = lax.dot_general(left, right, dims, preferred_element_type=jnp.float32)
                total = term if total is None else total + term
            if (row, col) == (1, 1):
                corner = total[T:, T:]
                shifted = swapped(corner)
                corner_parts = (shifted, turned(shifted), turned(corner))
            for n, (i, j) in enumerate(PARTS[h]):
                if i // 2 == row and j // 2 == col:
                    i0, j0 = (i % 2) * T, (j % 2) * T
                    block = total[i0:i0 + T, j0:j0 + T]
                    if i == j:
                        block = jnp.where(low_left(), corner_parts[i], block)
                    kept = part if c == 0 else last
                    kept[h][:, side, n] = block.reshape(16, 8, T)

    order = (2, 1, 3)

    def send_x(c):
        for k in order:
            x_copy(c, k).start()

    def arrive(c):
        own[c].wait()
        for k in order:
            x_copy(c, k).wait_recv()

    @pl.when(core == 1)
    def _():
        pl.semaphore_wait(turn, 1)

    send_x(0)
    for g in range(16):
        pick = jnp.int32(0)
        for j in range(16):
            pick = jnp.where(lax.shift_right_logical(table[f, j], 4) == g, j, pick)
        items[g] = pick
    lax.fori_loop(0, 16, find_column, 0)
    for axis, peers in enumerate((along_z, along_y, [across])):
        for peer in peers:
            pl.semaphore_signal(ready.at[axis], inc=1, device_id=peer, device_id_type=MESH)
        pl.semaphore_wait(ready.at[axis], len(peers))
    x_copy(0, 1).wait_send()
    pl.semaphore_signal(turn, inc=1, device_id=partner, device_id_type=MESH)

    arrive(0)
    for h in range(2):
        for side in range(2):
            gram(0, h, side)
        z_copy(h, 0).start()
    for h in range(2):
        z_copy(h, 0).wait_recv()
        part[h][pl.ds(b0 * 8, 8)] += r1[h][...]
        z_copy(h, 1).start()
    pl.semaphore_wait(turn, 1)
    send_x(1)
    for h in range(2):
        z_copy(h, 1).wait_recv()
        part[h][pl.ds(home, 4)] += r2[h][...]
        for k in order:
            t_copy(h, k).start()
        xt[h][pl.ds(4 * x, 2)] = part[h][piece]
    x_copy(1, 1).wait_send()

    @pl.when(core == 0)
    def _():
        pl.semaphore_signal(turn, inc=1, device_id=partner, device_id_type=MESH)

    arrive(1)
    for h in range(2):
        for side in range(2):
            gram(1, h, side)
        for e in others_d:
            w_copy(h, e).start()
        r3[h][d] = last[h][piece]
    for h in range(2):
        for k in order:
            t_copy(h, k).wait_recv()
    for h in range(2):
        for e in others_d:
            w_landed(h, e).wait_recv()
        for i in range(4):
            here = r3[h][4 * i:4 * i + 4]
            xt[h][4 * i + 2:4 * i + 4] = (here[0] + here[1]) + (here[2] + here[3])
        for g in others_f:
            fs[h][g] = xt[h][items[g]]
            a_copy(h, g).start()
        fr[h][f] = xt[h][items[f]]
    for h in range(2):
        for g in others_f:
            a_landed(h, g).wait_recv()
        for e in others_d:
            ds[h][e] = fr[h][columns[e]]
            b_copy(h, e).start()
        dr[h][piece] = fr[h][columns[d]]
    for h in range(2):
        for e in others_d:
            b_landed(h, e).wait_recv()
        out[h][...] = dr[h][...]

    for c in range(2):
        for k in (2, 3):
            x_copy(c, k).wait_send()
    for h in range(2):
        for step in range(2):
            z_copy(h, step).wait_send()
        for k in order:
            t_copy(h, k).wait_send()
        for e in others_d:
            w_copy(h, e).wait_send()
            b_copy(h, e).wait_send()
        for g in others_f:
            a_copy(h, g).wait_send()


def routed(table, grads):
    tiles = [(len(blocks), 8, T) for blocks in PARTS]

    def buffers(*lead):
        return [pltpu.VMEM(lead + tile, jnp.float32) for tile in tiles]

    def semaphores(*shape):
        return [pltpu.SemaphoreType.DMA(shape)] * 2

    return pl.pallas_call(
        route,
        out_shape=tuple(jax.ShapeDtypeStruct((16,) + tile, jnp.float32) for tile in tiles),
        in_specs=[
            pl.BlockSpec(memory_space=pltpu.SMEM),
            pl.BlockSpec(memory_space=pltpu.HBM),
        ],
        out_specs=(pl.BlockSpec(memory_space=pltpu.VMEM),) * 2,
        scratch_shapes=[
            pltpu.VMEM((2, 4, B, B), jnp.bfloat16),
            *buffers(16, 2),
            *buffers(16, 2),
            *buffers(8, 2),
            *buffers(4, 2),
            *buffers(16, 2),
            *buffers(16),
            *buffers(16),
            *buffers(16),
            *buffers(16),
            *buffers(16),
            pltpu.SMEM((16,), jnp.int32),
            pltpu.SMEM((16,), jnp.int32),
            pltpu.SemaphoreType.DMA((2,)),
            *semaphores(2, 4),
            *semaphores(2, 2),
            *semaphores(2, 16),
            *semaphores(2, 4),
            *semaphores(2, 16),
            *semaphores(2, 16),
            pltpu.SemaphoreType.REGULAR,
            pltpu.SemaphoreType.REGULAR((3,)),
        ],
        compiler_params=pltpu.CompilerParams(
            collective_id=0, has_side_effects=True, vmem_limit_bytes=52 * 1024 * 1024
        ),
        cost_estimate=pl.CostEstimate(flops=4 * 10**9, bytes_accessed=8 * 10**6, transcendentals=0),
        name="route",
    )(table, grads)


def split(a):
    high = a.astype(jnp.bfloat16)
    return high, (a - high.astype(jnp.float32)).astype(jnp.bfloat16)


def halves(matrix):
    return {place: split(quarter) for place, quarter in matrix.items()}


def product(a, b):
    out = {}
    for r, c in ((0, 0), (0, 1), (1, 1)):
        left, right = [], []
        for k in range(2):
            left += [a[r, k][0], a[r, k][0], a[r, k][1]]
            right += [b[k, c][0], b[k, c][1], b[k, c][0]]
        out[r, c] = jnp.dot(
            jnp.concatenate(left, axis=1), jnp.concatenate(right, axis=0), preferred_element_type=jnp.float32
        )
    out[1, 0] = out[0, 1].T
    return out


def newton(tri0, tri1, old, stats, roots):
    def blend(i, j, block):
        rows, cols = slice(i * T, (i + 1) * T), slice(j * T, (j + 1) * T)
        stats[rows, cols] = BETA * old[rows, cols] + (1.0 - BETA) * block

    mask = low_left()
    kept = []
    for tri, n, (i, j) in [(tri, n, p) for tri, ps in zip((tri0, tri1), PARTS) for n, p in enumerate(ps)]:
        block = tri[:, n].reshape(T, T)
        if i == j:
            kept.append(block)
            blend(i, i, jnp.where(mask, block.T, block))
        else:
            blend(i, j, block)
            blend(j, i, block.T)
    first, second, third = kept
    left = lax.broadcasted_iota(jnp.int32, (T // 2, T), 1) < T // 2
    top = jnp.where(left, first[T // 2:], turned(second[T // 2:]))
    corner = jnp.concatenate([top, turned(third[T // 2:])], axis=0)
    blend(3, 3, jnp.where(mask, corner.T, corner))

    scale = 2.5 / jnp.sqrt(jnp.sum(stats[...] * stats[...], keepdims=True) + 1e-06)
    eye = lax.broadcasted_iota(jnp.int32, (H, H), 0) == lax.broadcasted_iota(jnp.int32, (H, H), 1)

    def factor_of(matrix):
        return {
            (r, c): (jnp.where(eye, 1.25, 0.0) if r == c else 0.0) - 0.25 * quarter
            for (r, c), quarter in matrix.items()
        }

    moving = {
        (r, c): scale * stats[r * H:(r + 1) * H, c * H:(c + 1) * H] for r in range(2) for c in range(2)
    }
    root = factor_of(moving)
    factor = halves(root)
    for sweep in range(1, ITERS):
        square = halves(product(factor, factor))
        fourth = halves(product(square, square))
        moving = product(fourth, halves(moving))
        factor = halves(factor_of(moving))
        root = product(halves(root), factor)
    post = jnp.sqrt(jnp.sqrt(scale))
    for (r, c), quarter in root.items():
        roots[r * H:(r + 1) * H, c * H:(c + 1) * H] = post * quarter


def finished(tri0, tri1, old):
    whole = pl.BlockSpec(memory_space=pltpu.VMEM)
    return pl.pallas_call(
        newton,
        out_shape=(jax.ShapeDtypeStruct((B, B), jnp.float32),) * 2,
        in_specs=[whole] * 3,
        out_specs=(whole, whole),
        compiler_params=pltpu.CompilerParams(vmem_limit_bytes=48 * 1024 * 1024),
        cost_estimate=pl.CostEstimate(flops=13 * 10**9, bytes_accessed=4 * 10**6, transcendentals=0),
        name="newton",
    )(tri0, tri1, old)


def local(gradients, old_stats, owner_table):
    tri0, tri1 = routed(owner_table, gradients[0])
    stats, roots = finished(tri0, tri1, old_stats[0, 0])
    return (stats[None, None], roots[None, None])


def solution(mesh):
    placed = (P("dp", "factor", None, None), P("dp", "factor", None, None), P())
    return jax.shard_map(
        local,
        mesh=mesh,
        in_specs=placed,
        out_specs=(P("dp", "factor", None, None), P("dp", "factor", None, None)),
        check_vma=False,
    )
```

```python
import jax
import jax.numpy as jnp
from jax import lax
from jax.experimental import pallas as pl
from jax.experimental.pallas import tpu as pltpu
from jax.sharding import PartitionSpec as P

ITERS = 5
BETA = 0.9
B = 512
T = 128
MESH = pl.DeviceIdType.MESH
PARTS = (((0, 2), (0, 3), (1, 2), (1, 3)), ((0, 1), (2, 3), (0, 0), (1, 1), (2, 2)))
QUADS = (((0, 1),), ((1, 1), (0, 0)))
H = 256


def low_left():
    rows = lax.broadcasted_iota(jnp.int32, (T, T), 0)
    cols = lax.broadcasted_iota(jnp.int32, (T, T), 1)
    return jnp.logical_and(rows >= T // 2, cols < T // 2)


def swapped(block):
    return jnp.concatenate([block[T // 2:], block[:T // 2]], axis=0)


def turned(block):
    return jnp.concatenate([block[:, T // 2:], block[:, :T // 2]], axis=1)


def route(table, grads, out0, out1, xg, *refs):
    pairs = [(refs[2 * i], refs[2 * i + 1]) for i in range(11)]
    part, r1, r3 = ([pairs[2 * i], pairs[2 * i + 1]] for i in range(3))
    xt, fs, fr, ds, dr = pairs[6:]
    items, columns, own_sem, xs, xr, zs, zr, ws, wr, as_, ar, bs, br, turn, ready = refs[22:]
    out = (out0, out1)
    d = lax.axis_index("dp")
    f = lax.axis_index("factor")
    x, zl = d // 4, d % 4
    zh, y, core = f // 8, (f // 2) % 4, f % 2
    q = zl + zh * (3 - 2 * zl)
    b0, b1 = q % 2, q // 2
    piece = b0 * 8 + b1 * 4 + x

    def dp_at(x_, q_, zh_):
        return x_ * 4 + q_ + zh_ * (3 - 2 * q_)

    def x_peer(k):
        return {"dp": dp_at((x + k) % 4, q, zh), "factor": f}

    def f_peer(g):
        return {"dp": dp_at(x, q, g // 8), "factor": g}

    def d_peer(e):
        return {"dp": e, "factor": f}

    partner = {"dp": d, "factor": f + 1 - 2 * core}
    along_z = [{"dp": dp_at(x, (q + k) % 4, zh), "factor": f} for k in range(1, 4)]
    along_y = [{"dp": d, "factor": zh * 8 + ((y + k) % 4) * 2 + core} for k in range(1, 4)]
    across = {"dp": dp_at(x, q, 1 - zh), "factor": (1 - zh) * 8 + y * 2 + core}
    barrier = pltpu.get_barrier_semaphore()
    for peer in [x_peer(k) for k in range(1, 4)] + [partner] + along_z + along_y + [across]:
        pl.semaphore_signal(barrier, inc=1, device_id=peer, device_id_type=MESH)
    own = [pltpu.make_async_copy(grads.at[2 * x + c], xg.at[c, 0], own_sem.at[c]) for c in range(2)]
    for copy in own:
        copy.start()

    others_d = [dp_at((x + k // 2) % 4, (1 - b1) * 2 + k % 2, zh) for k in range(8)]
    others_d += [dp_at((x + k // 2) % 4, b1 * 2 + (b0 + k) % 2, zh) for k in range(1, 8)]
    others_f = [(1 - zh) * 8 + (f + k) % 8 for k in range(8)] + [zh * 8 + (f + k) % 8 for k in range(1, 8)]

    def find_column(e, carry):
        def scan(c, found):
            for j in range(16):
                found = jnp.where(table[c, j] == f * 16 + e, c, found)
            return found
        columns[e] = lax.fori_loop(0, 16, scan, jnp.int32(0))
        return carry

    pl.semaphore_wait(barrier, 11)

    def x_copy(c, k, half):
        rows = pl.ds(half * H, H)
        return pltpu.make_async_remote_copy(
            src_ref=grads.at[2 * ((x + k) % 4) + c, rows], dst_ref=xg.at[c, k, rows],
            send_sem=xs.at[c, k, half], recv_sem=xr.at[c, k, half], device_id=x_peer(k), device_id_type=MESH)

    def z_copy(c, h):
        return pltpu.make_async_remote_copy(
            src_ref=part[c][h].at[pl.ds((1 - b0) * 8, 8)], dst_ref=r1[c][h],
            send_sem=zs.at[c, h], recv_sem=zr.at[c, h],
            device_id={"dp": dp_at(x, q + 1 - 2 * b0, zh), "factor": f}, device_id_type=MESH)

    places = [((x + k) % 4, 1 - b1) for k in range(4)] + [((x + k) % 4, b1) for k in range(1, 4)]

    def w_copy(c, h, to):
        slot = to[0] * 2 + to[1]
        return pltpu.make_async_remote_copy(
            src_ref=part[c][h].at[b0 * 8 + to[1] * 4 + to[0]], dst_ref=r3[c][h].at[x * 2 + b1],
            send_sem=ws.at[c, h, slot], recv_sem=wr.at[c, h, x * 2 + b1],
            device_id={"dp": dp_at(to[0], b0 + 2 * to[1], zh), "factor": f}, device_id_type=MESH)

    def w_landed(c, h, to):
        slot = to[0] * 2 + to[1]
        return pltpu.make_async_remote_copy(
            src_ref=part[c][h].at[b0 * 8 + to[1] * 4 + to[0]], dst_ref=r3[c][h].at[slot],
            send_sem=ws.at[c, h, slot], recv_sem=wr.at[c, h, slot],
            device_id={"dp": dp_at(to[0], b0 + 2 * to[1], zh), "factor": f}, device_id_type=MESH)

    def piece_of(e):
        e_x, e_zl = e // 4, e % 4
        e_q = e_zl + zh * (3 - 2 * e_zl)
        return (e_q % 2) * 8 + (e_q // 2) * 4 + e_x

    def a_copy(h, g):
        return pltpu.make_async_remote_copy(
            src_ref=fs[h].at[g], dst_ref=fr[h].at[f], send_sem=as_.at[h, g], recv_sem=ar.at[h, f],
            device_id=f_peer(g), device_id_type=MESH)

    def a_landed(h, g):
        return pltpu.make_async_remote_copy(
            src_ref=fs[h].at[g], dst_ref=fr[h].at[g], send_sem=as_.at[h, g], recv_sem=ar.at[h, g],
            device_id=f_peer(g), device_id_type=MESH)

    def b_copy(h, e):
        return pltpu.make_async_remote_copy(
            src_ref=ds[h].at[e], dst_ref=dr[h].at[piece], send_sem=bs.at[h, e], recv_sem=br.at[h, piece],
            device_id=d_peer(e), device_id_type=MESH)

    def b_landed(h, e):
        e_piece = piece_of(e)
        return pltpu.make_async_remote_copy(
            src_ref=ds[h].at[e], dst_ref=dr[h].at[e_piece], send_sem=bs.at[h, e], recv_sem=br.at[h, e_piece],
            device_id=d_peer(e), device_id_type=MESH)

    def gram(c, h, side):
        corner = None
        for row, col in QUADS[h]:
            total = None
            for k in range(4):
                if side == 0:
                    left = xg[c, k, row * H:(row + 1) * H, :]
                    right = xg[c, k, col * H:(col + 1) * H, :]
                    dims = (((1,), (1,)), ((), ()))
                else:
                    left = xg[c, k, :, row * H:(row + 1) * H]
                    right = xg[c, k, :, col * H:(col + 1) * H]
                    dims = (((0,), (0,)), ((), ()))
                term = lax.dot_general(left, right, dims, preferred_element_type=jnp.float32)
                total = term if total is None else total + term
            if (row, col) == (1, 1):
                corner = total[T:, T:]
                shifted = swapped(corner)
                corner_parts = (shifted, turned(shifted), turned(corner))
            for n, (i, j) in enumerate(PARTS[h]):
                if i // 2 == row and j // 2 == col:
                    i0, j0 = (i % 2) * T, (j % 2) * T
                    block = total[i0:i0 + T, j0:j0 + T]
                    if i == j:
                        block = jnp.where(low_left(), corner_parts[i], block)
                    part[c][h][:, side, n] = block.reshape(16, 8, T)

    order = (2, 1, 3)

    def send_x(c):
        for half in range(2):
            for k in order:
                x_copy(c, k, half).start()

    def half_sent(c):
        for k in order:
            x_copy(c, k, 0).wait_send()

    def arrive(c):
        own[c].wait()
        for half in range(2):
            for k in order:
                x_copy(c, k, half).wait_recv()
        for h in range(2):
            for side in range(2):
                gram(c, h, side)
            z_copy(c, h).start()

    def pass_on(c, h):
        z_copy(c, h).wait_recv()
        part[c][h][pl.ds(b0 * 8, 8)] += r1[c][h][...]
        for to in places:
            w_copy(c, h, to).start()
        r3[c][h][x * 2 + b1] = part[c][h][piece]

    def settle(c, h):
        for to in places:
            w_landed(c, h, to).wait_recv()
        for i in range(4):
            xt[h][4 * i + 2 * c:4 * i + 2 * c + 2] = r3[c][h][2 * i] + r3[c][h][2 * i + 1]

    @pl.when(core == 1)
    def _():
        pl.semaphore_wait(turn, 1)

    send_x(0)
    for g in range(16):
        pick = jnp.int32(0)
        for j in range(16):
            pick = jnp.where(lax.shift_right_logical(table[f, j], 4) == g, j, pick)
        items[g] = pick
    half_sent(0)
    pl.semaphore_signal(turn, inc=1, device_id=partner, device_id_type=MESH)
    lax.fori_loop(0, 16, find_column, 0)
    for axis, peers in enumerate((along_z, along_y, [across])):
        for peer in peers:
            pl.semaphore_signal(ready.at[axis], inc=1, device_id=peer, device_id_type=MESH)
        pl.semaphore_wait(ready.at[axis], len(peers))

    arrive(0)
    pl.semaphore_wait(turn, 1)
    send_x(1)
    for h in range(2):
        pass_on(0, h)
    half_sent(1)

    @pl.when(core == 0)
    def _():
        pl.semaphore_signal(turn, inc=1, device_id=partner, device_id_type=MESH)

    arrive(1)
    for h in range(2):
        settle(0, h)
    for h in range(2):
        pass_on(1, h)
    for h in range(2):
        settle(1, h)
        for g in others_f:
            fs[h][g] = xt[h][items[g]]
            a_copy(h, g).start()
        fr[h][f] = xt[h][items[f]]
    for h in range(2):
        for g in others_f:
            a_landed(h, g).wait_recv()
        for e in others_d:
            ds[h][e] = fr[h][columns[e]]
            b_copy(h, e).start()
        dr[h][piece] = fr[h][columns[d]]
    for h in range(2):
        for e in others_d:
            b_landed(h, e).wait_recv()
        out[h][...] = dr[h][...]

    for c in range(2):
        for k in order:
            x_copy(c, k, 1).wait_send()
        for h in range(2):
            z_copy(c, h).wait_send()
            for to in places:
                w_copy(c, h, to).wait_send()
    for h in range(2):
        for e in others_d:
            b_copy(h, e).wait_send()
        for g in others_f:
            a_copy(h, g).wait_send()


def routed(table, grads):
    tiles = [(len(blocks), 8, T) for blocks in PARTS]

    def buffers(*lead):
        return [pltpu.VMEM(lead + tile, jnp.float32) for tile in tiles]

    def semaphores(*shape):
        return [pltpu.SemaphoreType.DMA(shape)] * 2

    return pl.pallas_call(
        route,
        out_shape=tuple(jax.ShapeDtypeStruct((16,) + tile, jnp.float32) for tile in tiles),
        in_specs=[
            pl.BlockSpec(memory_space=pltpu.SMEM),
            pl.BlockSpec(memory_space=pltpu.HBM),
        ],
        out_specs=(pl.BlockSpec(memory_space=pltpu.VMEM),) * 2,
        scratch_shapes=[
            pltpu.VMEM((2, 4, B, B), jnp.bfloat16),
            *buffers(16, 2) * 2,
            *buffers(8, 2) * 2,
            *buffers(8, 2) * 2,
            *buffers(16) * 5,
            pltpu.SMEM((16,), jnp.int32),
            pltpu.SMEM((16,), jnp.int32),
            pltpu.SemaphoreType.DMA((2,)),
            *semaphores(2, 4, 2),
            *semaphores(2, 2),
            *semaphores(2, 2, 8),
            *semaphores(2, 16),
            *semaphores(2, 16),
            pltpu.SemaphoreType.REGULAR,
            pltpu.SemaphoreType.REGULAR((3,)),
        ],
        compiler_params=pltpu.CompilerParams(
            collective_id=0, has_side_effects=True, vmem_limit_bytes=52 * 1024 * 1024
        ),
        cost_estimate=pl.CostEstimate(flops=4 * 10**9, bytes_accessed=8 * 10**6, transcendentals=0),
        name="route",
    )(table, grads)


def split(a):
    high = a.astype(jnp.bfloat16)
    return high, (a - high.astype(jnp.float32)).astype(jnp.bfloat16)


def halves(matrix):
    return {place: split(quarter) for place, quarter in matrix.items()}


def product(a, b):
    out = {}
    for r, c in ((0, 0), (0, 1), (1, 1)):
        left, right = [], []
        for k in range(2):
            left += [a[r, k][0], a[r, k][0], a[r, k][1]]
            right += [b[k, c][0], b[k, c][1], b[k, c][0]]
        out[r, c] = jnp.dot(
            jnp.concatenate(left, axis=1), jnp.concatenate(right, axis=0), preferred_element_type=jnp.float32
        )
    out[1, 0] = out[0, 1].T
    return out


def newton(tri0, tri1, old, stats, roots):
    def blend(i, j, block):
        rows, cols = slice(i * T, (i + 1) * T), slice(j * T, (j + 1) * T)
        stats[rows, cols] = BETA * old[rows, cols] + (1.0 - BETA) * block

    mask = low_left()
    kept = []
    for tri, n, (i, j) in [(tri, n, p) for tri, ps in zip((tri0, tri1), PARTS) for n, p in enumerate(ps)]:
        block = tri[:, n].reshape(T, T)
        if i == j:
            kept.append(block)
            blend(i, i, jnp.where(mask, block.T, block))
        else:
            blend(i, j, block)
            blend(j, i, block.T)
    first, second, third = kept
    left = lax.broadcasted_iota(jnp.int32, (T // 2, T), 1) < T // 2
    top = jnp.where(left, first[T // 2:], turned(second[T // 2:]))
    corner = jnp.concatenate([top, turned(third[T // 2:])], axis=0)
    blend(3, 3, jnp.where(mask, corner.T, corner))

    scale = 2.5 / jnp.sqrt(jnp.sum(stats[...] * stats[...], keepdims=True) + 1e-06)
    eye = lax.broadcasted_iota(jnp.int32, (H, H), 0) == lax.broadcasted_iota(jnp.int32, (H, H), 1)

    def factor_of(matrix):
        return {
            (r, c): (jnp.where(eye, 1.25, 0.0) if r == c else 0.0) - 0.25 * quarter
            for (r, c), quarter in matrix.items()
        }

    moving = {
        (r, c): scale * stats[r * H:(r + 1) * H, c * H:(c + 1) * H] for r in range(2) for c in range(2)
    }
    root = factor_of(moving)
    factor = halves(root)
    for sweep in range(1, ITERS):
        square = halves(product(factor, factor))
        fourth = halves(product(square, square))
        moving = product(fourth, halves(moving))
        factor = halves(factor_of(moving))
        root = product(halves(root), factor)
    post = jnp.sqrt(jnp.sqrt(scale))
    for (r, c), quarter in root.items():
        roots[r * H:(r + 1) * H, c * H:(c + 1) * H] = post * quarter


def finished(tri0, tri1, old):
    whole = pl.BlockSpec(memory_space=pltpu.VMEM)
    return pl.pallas_call(
        newton,
        out_shape=(jax.ShapeDtypeStruct((B, B), jnp.float32),) * 2,
        in_specs=[whole] * 3,
        out_specs=(whole, whole),
        compiler_params=pltpu.CompilerParams(vmem_limit_bytes=48 * 1024 * 1024),
        cost_estimate=pl.CostEstimate(flops=13 * 10**9, bytes_accessed=4 * 10**6, transcendentals=0),
        name="newton",
    )(tri0, tri1, old)


def local(gradients, old_stats, owner_table):
    tri0, tri1 = routed(owner_table, gradients[0])
    stats, roots = finished(tri0, tri1, old_stats[0, 0])
    return (stats[None, None], roots[None, None])


def solution(mesh):
    placed = (P("dp", "factor", None, None), P("dp", "factor", None, None), P())
    return jax.shard_map(
        local,
        mesh=mesh,
        in_specs=placed,
        out_specs=(P("dp", "factor", None, None), P("dp", "factor", None, None)),
        check_vma=False,
    )
```

```python
import jax
import jax.numpy as jnp
from jax import lax
from jax.experimental import pallas as pl
from jax.experimental.pallas import tpu as pltpu
from jax.sharding import PartitionSpec as P

ITERS = 5
BETA = 0.9
B = 512
T = 128
MESH = pl.DeviceIdType.MESH
PARTS = (((0, 2), (0, 3), (1, 2), (1, 3)), ((0, 1), (2, 3), (0, 0), (1, 1), (2, 2)))
QUADS = (((0, 1),), ((1, 1), (0, 0)))
H = 256


def low_left():
    rows = lax.broadcasted_iota(jnp.int32, (T, T), 0)
    cols = lax.broadcasted_iota(jnp.int32, (T, T), 1)
    return jnp.logical_and(rows >= T // 2, cols < T // 2)


def swapped(block):
    return jnp.concatenate([block[T // 2:], block[:T // 2]], axis=0)


def turned(block):
    return jnp.concatenate([block[:, T // 2:], block[:, :T // 2]], axis=1)


def route(table, grads, out0, out1, xg, *refs):
    pairs = [(refs[2 * i], refs[2 * i + 1]) for i in range(11)]
    part, r1, r3 = ([pairs[2 * i], pairs[2 * i + 1]] for i in range(3))
    xt, fs, fr, ds, dr = pairs[6:]
    items, columns, own_sem, xs, xr, zs, zr, ws, wr, as_, ar, bs, br, turn, ready = refs[22:]
    out = (out0, out1)
    d = lax.axis_index("dp")
    f = lax.axis_index("factor")
    x, zl = d // 4, d % 4
    zh, y, core = f // 8, (f // 2) % 4, f % 2
    q = zl + zh * (3 - 2 * zl)
    b0, b1 = q % 2, q // 2
    piece = b0 * 8 + b1 * 4 + x

    def dp_at(x_, q_, zh_):
        return x_ * 4 + q_ + zh_ * (3 - 2 * q_)

    def x_peer(k):
        return {"dp": dp_at((x + k) % 4, q, zh), "factor": f}

    def f_peer(g):
        return {"dp": dp_at(x, q, g // 8), "factor": g}

    def d_peer(e):
        return {"dp": e, "factor": f}

    partner = {"dp": d, "factor": f + 1 - 2 * core}
    along_z = [{"dp": dp_at(x, (q + k) % 4, zh), "factor": f} for k in range(1, 4)]
    along_y = [{"dp": d, "factor": zh * 8 + ((y + k) % 4) * 2 + core} for k in range(1, 4)]
    across = {"dp": dp_at(x, q, 1 - zh), "factor": (1 - zh) * 8 + y * 2 + core}
    barrier = pltpu.get_barrier_semaphore()
    for peer in [x_peer(k) for k in range(1, 4)] + [partner] + along_z + along_y + [across]:
        pl.semaphore_signal(barrier, inc=1, device_id=peer, device_id_type=MESH)
    own = [pltpu.make_async_copy(grads.at[2 * x + c], xg.at[c, 0], own_sem.at[c]) for c in range(2)]
    for copy in own:
        copy.start()

    others_d = [(d + k) % 16 for k in range(1, 16)]
    others_f = [(f + k) % 16 for k in range(1, 16)]

    def find_column(e, carry):
        def scan(c, found):
            for j in range(16):
                found = jnp.where(table[c, j] == f * 16 + e, c, found)
            return found
        columns[e] = lax.fori_loop(0, 16, scan, jnp.int32(0))
        return carry

    pl.semaphore_wait(barrier, 11)

    def x_copy(c, k, half):
        rows = pl.ds(half * H, H)
        return pltpu.make_async_remote_copy(
            src_ref=grads.at[2 * ((x + k) % 4) + c, rows], dst_ref=xg.at[c, k, rows],
            send_sem=xs.at[c, k, half], recv_sem=xr.at[c, k, half], device_id=x_peer(k), device_id_type=MESH)

    def z_copy(c, h):
        return pltpu.make_async_remote_copy(
            src_ref=part[c][h].at[pl.ds((1 - b0) * 8, 8)], dst_ref=r1[c][h],
            send_sem=zs.at[c, h], recv_sem=zr.at[c, h],
            device_id={"dp": dp_at(x, q + 1 - 2 * b0, zh), "factor": f}, device_id_type=MESH)

    places = [((x + k) % 4, up) for k in range(1, 4) for up in (1 - b1, b1)] + [(x, 1 - b1)]

    def w_copy(c, h, to):
        slot = to[0] * 2 + to[1]
        return pltpu.make_async_remote_copy(
            src_ref=part[c][h].at[b0 * 8 + to[1] * 4 + to[0]], dst_ref=r3[c][h].at[x * 2 + b1],
            send_sem=ws.at[c, h, slot], recv_sem=wr.at[c, h, x * 2 + b1],
            device_id={"dp": dp_at(to[0], b0 + 2 * to[1], zh), "factor": f}, device_id_type=MESH)

    def w_landed(c, h, to):
        slot = to[0] * 2 + to[1]
        return pltpu.make_async_remote_copy(
            src_ref=part[c][h].at[b0 * 8 + to[1] * 4 + to[0]], dst_ref=r3[c][h].at[slot],
            send_sem=ws.at[c, h, slot], recv_sem=wr.at[c, h, slot],
            device_id={"dp": dp_at(to[0], b0 + 2 * to[1], zh), "factor": f}, device_id_type=MESH)

    def piece_of(e):
        e_x, e_zl = e // 4, e % 4
        e_q = e_zl + zh * (3 - 2 * e_zl)
        return (e_q % 2) * 8 + (e_q // 2) * 4 + e_x

    def a_copy(h, g):
        return pltpu.make_async_remote_copy(
            src_ref=fs[h].at[g], dst_ref=fr[h].at[f], send_sem=as_.at[h, g], recv_sem=ar.at[h, f],
            device_id=f_peer(g), device_id_type=MESH)

    def a_landed(h, g):
        return pltpu.make_async_remote_copy(
            src_ref=fs[h].at[g], dst_ref=fr[h].at[g], send_sem=as_.at[h, g], recv_sem=ar.at[h, g],
            device_id=f_peer(g), device_id_type=MESH)

    def b_copy(h, e):
        return pltpu.make_async_remote_copy(
            src_ref=ds[h].at[e], dst_ref=dr[h].at[piece], send_sem=bs.at[h, e], recv_sem=br.at[h, piece],
            device_id=d_peer(e), device_id_type=MESH)

    def b_landed(h, e):
        e_piece = piece_of(e)
        return pltpu.make_async_remote_copy(
            src_ref=ds[h].at[e], dst_ref=dr[h].at[e_piece], send_sem=bs.at[h, e], recv_sem=br.at[h, e_piece],
            device_id=d_peer(e), device_id_type=MESH)

    def gram(c, h, side):
        corner = None
        for row, col in QUADS[h]:
            total = None
            for k in range(4):
                if side == 0:
                    left = xg[c, k, row * H:(row + 1) * H, :]
                    right = xg[c, k, col * H:(col + 1) * H, :]
                    dims = (((1,), (1,)), ((), ()))
                else:
                    left = xg[c, k, :, row * H:(row + 1) * H]
                    right = xg[c, k, :, col * H:(col + 1) * H]
                    dims = (((0,), (0,)), ((), ()))
                term = lax.dot_general(left, right, dims, preferred_element_type=jnp.float32)
                total = term if total is None else total + term
            if (row, col) == (1, 1):
                corner = total[T:, T:]
                shifted = swapped(corner)
                corner_parts = (shifted, turned(shifted), turned(corner))
            for n, (i, j) in enumerate(PARTS[h]):
                if i // 2 == row and j // 2 == col:
                    i0, j0 = (i % 2) * T, (j % 2) * T
                    block = total[i0:i0 + T, j0:j0 + T]
                    if i == j:
                        block = jnp.where(low_left(), corner_parts[i], block)
                    part[c][h][:, side, n] = block.reshape(16, 8, T)

    order = (2, 1, 3)

    def send_x(c):
        for half in range(2):
            for k in order:
                x_copy(c, k, half).start()

    def half_sent(c):
        for k in order:
            x_copy(c, k, 0).wait_send()

    def arrive(c):
        own[c].wait()
        for half in range(2):
            for k in order:
                x_copy(c, k, half).wait_recv()
        for h in range(2):
            for side in range(2):
                gram(c, h, side)
            z_copy(c, h).start()

    def pass_on(c, h):
        z_copy(c, h).wait_recv()
        part[c][h][pl.ds(b0 * 8, 8)] += r1[c][h][...]
        for to in places:
            w_copy(c, h, to).start()
        r3[c][h][x * 2 + b1] = part[c][h][piece]

    def settle(c, h):
        for to in places:
            w_landed(c, h, to).wait_recv()
        for i in range(4):
            xt[h][4 * i + 2 * c:4 * i + 2 * c + 2] = r3[c][h][2 * i] + r3[c][h][2 * i + 1]

    @pl.when(core == 1)
    def _():
        pl.semaphore_wait(turn, 1)

    send_x(0)
    for g in range(16):
        pick = jnp.int32(0)
        for j in range(16):
            pick = jnp.where(lax.shift_right_logical(table[f, j], 4) == g, j, pick)
        items[g] = pick
    half_sent(0)
    pl.semaphore_signal(turn, inc=1, device_id=partner, device_id_type=MESH)
    lax.fori_loop(0, 16, find_column, 0)
    for axis, peers in enumerate((along_z, along_y, [across])):
        for peer in peers:
            pl.semaphore_signal(ready.at[axis], inc=1, device_id=peer, device_id_type=MESH)
        pl.semaphore_wait(ready.at[axis], len(peers))

    arrive(0)
    pl.semaphore_wait(turn, 1)
    send_x(1)
    for h in range(2):
        pass_on(0, h)
    half_sent(1)

    @pl.when(core == 0)
    def _():
        pl.semaphore_signal(turn, inc=1, device_id=partner, device_id_type=MESH)

    arrive(1)
    for h in range(2):
        settle(0, h)
    for h in range(2):
        pass_on(1, h)
    for h in range(2):
        settle(1, h)
        for g in others_f:
            fs[h][g] = xt[h][items[g]]
            a_copy(h, g).start()
        fr[h][f] = xt[h][items[f]]
    for h in range(2):
        for g in others_f:
            a_landed(h, g).wait_recv()
        for e in others_d:
            ds[h][e] = fr[h][columns[e]]
            b_copy(h, e).start()
        dr[h][piece] = fr[h][columns[d]]
    for h in range(2):
        for e in others_d:
            b_landed(h, e).wait_recv()
        out[h][...] = dr[h][...]

    for c in range(2):
        for k in order:
            x_copy(c, k, 1).wait_send()
        for h in range(2):
            z_copy(c, h).wait_send()
            for to in places:
                w_copy(c, h, to).wait_send()
    for h in range(2):
        for e in others_d:
            b_copy(h, e).wait_send()
        for g in others_f:
            a_copy(h, g).wait_send()


def routed(table, grads):
    tiles = [(len(blocks), 8, T) for blocks in PARTS]

    def buffers(*lead):
        return [pltpu.VMEM(lead + tile, jnp.float32) for tile in tiles]

    def semaphores(*shape):
        return [pltpu.SemaphoreType.DMA(shape)] * 2

    return pl.pallas_call(
        route,
        out_shape=tuple(jax.ShapeDtypeStruct((16,) + tile, jnp.float32) for tile in tiles),
        in_specs=[
            pl.BlockSpec(memory_space=pltpu.SMEM),
            pl.BlockSpec(memory_space=pltpu.HBM),
        ],
        out_specs=(pl.BlockSpec(memory_space=pltpu.VMEM),) * 2,
        scratch_shapes=[
            pltpu.VMEM((2, 4, B, B), jnp.bfloat16),
            *buffers(16, 2) * 2,
            *buffers(8, 2) * 2,
            *buffers(8, 2) * 2,
            *buffers(16) * 5,
            pltpu.SMEM((16,), jnp.int32),
            pltpu.SMEM((16,), jnp.int32),
            pltpu.SemaphoreType.DMA((2,)),
            *semaphores(2, 4, 2),
            *semaphores(2, 2),
            *semaphores(2, 2, 8),
            *semaphores(2, 16),
            *semaphores(2, 16),
            pltpu.SemaphoreType.REGULAR,
            pltpu.SemaphoreType.REGULAR((3,)),
        ],
        compiler_params=pltpu.CompilerParams(
            collective_id=0, has_side_effects=True, vmem_limit_bytes=52 * 1024 * 1024
        ),
        cost_estimate=pl.CostEstimate(flops=4 * 10**9, bytes_accessed=8 * 10**6, transcendentals=0),
        name="route",
    )(table, grads)


def split(a):
    high = a.astype(jnp.bfloat16)
    return high, (a - high.astype(jnp.float32)).astype(jnp.bfloat16)


def halves(matrix):
    return {place: split(quarter) for place, quarter in matrix.items()}


def product(a, b):
    out = {}
    for r, c in ((0, 0), (0, 1), (1, 1)):
        left, right = [], []
        for k in range(2):
            left += [a[r, k][0], a[r, k][0], a[r, k][1]]
            right += [b[k, c][0], b[k, c][1], b[k, c][0]]
        out[r, c] = jnp.dot(
            jnp.concatenate(left, axis=1), jnp.concatenate(right, axis=0), preferred_element_type=jnp.float32
        )
    out[1, 0] = out[0, 1].T
    return out


def newton(tri0, tri1, old, stats, roots):
    def blend(i, j, block):
        rows, cols = slice(i * T, (i + 1) * T), slice(j * T, (j + 1) * T)
        stats[rows, cols] = BETA * old[rows, cols] + (1.0 - BETA) * block

    mask = low_left()
    kept = []
    for tri, n, (i, j) in [(tri, n, p) for tri, ps in zip((tri0, tri1), PARTS) for n, p in enumerate(ps)]:
        block = tri[:, n].reshape(T, T)
        if i == j:
            kept.append(block)
            blend(i, i, jnp.where(mask, block.T, block))
        else:
            blend(i, j, block)
            blend(j, i, block.T)
    first, second, third = kept
    left = lax.broadcasted_iota(jnp.int32, (T // 2, T), 1) < T // 2
    top = jnp.where(left, first[T // 2:], turned(second[T // 2:]))
    corner = jnp.concatenate([top, turned(third[T // 2:])], axis=0)
    blend(3, 3, jnp.where(mask, corner.T, corner))

    scale = 2.5 / jnp.sqrt(jnp.sum(stats[...] * stats[...], keepdims=True) + 1e-06)
    eye = lax.broadcasted_iota(jnp.int32, (H, H), 0) == lax.broadcasted_iota(jnp.int32, (H, H), 1)

    def factor_of(matrix):
        return {
            (r, c): (jnp.where(eye, 1.25, 0.0) if r == c else 0.0) - 0.25 * quarter
            for (r, c), quarter in matrix.items()
        }

    moving = {
        (r, c): scale * stats[r * H:(r + 1) * H, c * H:(c + 1) * H] for r in range(2) for c in range(2)
    }
    root = factor_of(moving)
    factor = halves(root)
    for sweep in range(1, ITERS):
        square = halves(product(factor, factor))
        fourth = halves(product(square, square))
        moving = product(fourth, halves(moving))
        factor = halves(factor_of(moving))
        root = product(halves(root), factor)
    post = jnp.sqrt(jnp.sqrt(scale))
    for (r, c), quarter in root.items():
        roots[r * H:(r + 1) * H, c * H:(c + 1) * H] = post * quarter


def finished(tri0, tri1, old):
    whole = pl.BlockSpec(memory_space=pltpu.VMEM)
    return pl.pallas_call(
        newton,
        out_shape=(jax.ShapeDtypeStruct((B, B), jnp.float32),) * 2,
        in_specs=[whole] * 3,
        out_specs=(whole, whole),
        compiler_params=pltpu.CompilerParams(vmem_limit_bytes=48 * 1024 * 1024),
        cost_estimate=pl.CostEstimate(flops=13 * 10**9, bytes_accessed=4 * 10**6, transcendentals=0),
        name="newton",
    )(tri0, tri1, old)


def local(gradients, old_stats, owner_table):
    tri0, tri1 = routed(owner_table, gradients[0])
    stats, roots = finished(tri0, tri1, old_stats[0, 0])
    return (stats[None, None], roots[None, None])


def solution(mesh):
    placed = (P("dp", "factor", None, None), P("dp", "factor", None, None), P())
    return jax.shard_map(
        local,
        mesh=mesh,
        in_specs=placed,
        out_specs=(P("dp", "factor", None, None), P("dp", "factor", None, None)),
        check_vma=False,
    )
```

```python
import jax
import jax.numpy as jnp
from jax import lax
from jax.experimental import pallas as pl
from jax.experimental.pallas import tpu as pltpu
from jax.sharding import PartitionSpec as P

ITERS = 5
BETA = 0.9
B = 512
T = 128
MESH = pl.DeviceIdType.MESH
PARTS = (((0, 2), (0, 3), (1, 2), (1, 3)), ((0, 1), (2, 3), (0, 0), (1, 1), (2, 2)))
QUADS = (((0, 1),), ((1, 1), (0, 0)))
H = 256


def low_left():
    rows = lax.broadcasted_iota(jnp.int32, (T, T), 0)
    cols = lax.broadcasted_iota(jnp.int32, (T, T), 1)
    return jnp.logical_and(rows >= T // 2, cols < T // 2)


def swapped(block):
    return jnp.concatenate([block[T // 2:], block[:T // 2]], axis=0)


def turned(block):
    return jnp.concatenate([block[:, T // 2:], block[:, :T // 2]], axis=1)


def route(table, grads, out0, out1, xg, *refs):
    pairs = [(refs[2 * i], refs[2 * i + 1]) for i in range(11)]
    part, r1, r3 = ([pairs[2 * i], pairs[2 * i + 1]] for i in range(3))
    xt, fs, fr, ds, dr = pairs[6:]
    items, columns, own_sem, xs, xr, zs, zr, ws, wr, as_, ar, bs, br, turn, ready = refs[22:]
    out = (out0, out1)
    d = lax.axis_index("dp")
    f = lax.axis_index("factor")
    x, zl = d // 4, d % 4
    zh, y, core = f // 8, (f // 2) % 4, f % 2
    q = zl + zh * (3 - 2 * zl)
    b0, b1 = q % 2, q // 2
    piece = b0 * 8 + b1 * 4 + x

    def dp_at(x_, q_, zh_):
        return x_ * 4 + q_ + zh_ * (3 - 2 * q_)

    def x_peer(k):
        return {"dp": dp_at((x + k) % 4, q, zh), "factor": f}

    def f_peer(g):
        return {"dp": dp_at(x, q, g // 8), "factor": g}

    def d_peer(e):
        return {"dp": e, "factor": f}

    partner = {"dp": d, "factor": f + 1 - 2 * core}
    along_z = [{"dp": dp_at(x, (q + k) % 4, zh), "factor": f} for k in range(1, 4)]
    along_y = [{"dp": d, "factor": zh * 8 + ((y + k) % 4) * 2 + core} for k in range(1, 4)]
    across = {"dp": dp_at(x, q, 1 - zh), "factor": (1 - zh) * 8 + y * 2 + core}
    barrier = pltpu.get_barrier_semaphore()
    for peer in [x_peer(k) for k in range(1, 4)] + [partner] + along_z + along_y + [across]:
        pl.semaphore_signal(barrier, inc=1, device_id=peer, device_id_type=MESH)
    own = [pltpu.make_async_copy(grads.at[2 * x + c], xg.at[c, 0], own_sem.at[c]) for c in range(2)]
    for copy in own:
        copy.start()

    others_d = [(d + k) % 16 for k in range(1, 16)]
    others_f = [(f + k) % 16 for k in range(1, 16)]

    def find_column(e, carry):
        def scan(c, found):
            for j in range(16):
                found = jnp.where(table[c, j] == f * 16 + e, c, found)
            return found
        columns[e] = lax.fori_loop(0, 16, scan, jnp.int32(0))
        return carry

    pl.semaphore_wait(barrier, 11)

    def x_copy(c, k, half):
        rows = pl.ds(half * H, H)
        return pltpu.make_async_remote_copy(
            src_ref=grads.at[2 * ((x + k) % 4) + c, rows], dst_ref=xg.at[c, k, rows],
            send_sem=xs.at[c, k, half], recv_sem=xr.at[c, k, half], device_id=x_peer(k), device_id_type=MESH)

    def z_copy(c, h):
        return pltpu.make_async_remote_copy(
            src_ref=part[c][h].at[pl.ds((1 - b0) * 8, 8)], dst_ref=r1[c][h],
            send_sem=zs.at[c, h], recv_sem=zr.at[c, h],
            device_id={"dp": dp_at(x, q + 1 - 2 * b0, zh), "factor": f}, device_id_type=MESH)

    places = [((x + k) % 4, up) for k in range(1, 4) for up in (1 - b1, b1)] + [(x, 1 - b1)]

    def w_copy(c, h, to):
        slot = to[0] * 2 + to[1]
        return pltpu.make_async_remote_copy(
            src_ref=part[c][h].at[b0 * 8 + to[1] * 4 + to[0]], dst_ref=r3[c][h].at[x * 2 + b1],
            send_sem=ws.at[c, h, slot], recv_sem=wr.at[c, h, x * 2 + b1],
            device_id={"dp": dp_at(to[0], b0 + 2 * to[1], zh), "factor": f}, device_id_type=MESH)

    def w_landed(c, h, to):
        slot = to[0] * 2 + to[1]
        return pltpu.make_async_remote_copy(
            src_ref=part[c][h].at[b0 * 8 + to[1] * 4 + to[0]], dst_ref=r3[c][h].at[slot],
            send_sem=ws.at[c, h, slot], recv_sem=wr.at[c, h, slot],
            device_id={"dp": dp_at(to[0], b0 + 2 * to[1], zh), "factor": f}, device_id_type=MESH)

    def piece_of(e):
        e_x, e_zl = e // 4, e % 4
        e_q = e_zl + zh * (3 - 2 * e_zl)
        return (e_q % 2) * 8 + (e_q // 2) * 4 + e_x

    def a_copy(h, g):
        return pltpu.make_async_remote_copy(
            src_ref=fs[h].at[g], dst_ref=fr[h].at[f], send_sem=as_.at[h, g], recv_sem=ar.at[h, f],
            device_id=f_peer(g), device_id_type=MESH)

    def a_landed(h, g):
        return pltpu.make_async_remote_copy(
            src_ref=fs[h].at[g], dst_ref=fr[h].at[g], send_sem=as_.at[h, g], recv_sem=ar.at[h, g],
            device_id=f_peer(g), device_id_type=MESH)

    def b_copy(h, e):
        return pltpu.make_async_remote_copy(
            src_ref=ds[h].at[e], dst_ref=dr[h].at[piece], send_sem=bs.at[h, e], recv_sem=br.at[h, piece],
            device_id=d_peer(e), device_id_type=MESH)

    def b_landed(h, e):
        e_piece = piece_of(e)
        return pltpu.make_async_remote_copy(
            src_ref=ds[h].at[e], dst_ref=dr[h].at[e_piece], send_sem=bs.at[h, e], recv_sem=br.at[h, e_piece],
            device_id=d_peer(e), device_id_type=MESH)

    def gram(c, h, side):
        corner = None
        for row, col in QUADS[h]:
            total = None
            for k in range(4):
                if side == 0:
                    left = xg[c, k, row * H:(row + 1) * H, :]
                    right = xg[c, k, col * H:(col + 1) * H, :]
                    dims = (((1,), (1,)), ((), ()))
                else:
                    left = xg[c, k, :, row * H:(row + 1) * H]
                    right = xg[c, k, :, col * H:(col + 1) * H]
                    dims = (((0,), (0,)), ((), ()))
                term = lax.dot_general(left, right, dims, preferred_element_type=jnp.float32)
                total = term if total is None else total + term
            if (row, col) == (1, 1):
                corner = total[T:, T:]
                shifted = swapped(corner)
                corner_parts = (shifted, turned(shifted), turned(corner))
            for n, (i, j) in enumerate(PARTS[h]):
                if i // 2 == row and j // 2 == col:
                    i0, j0 = (i % 2) * T, (j % 2) * T
                    block = total[i0:i0 + T, j0:j0 + T]
                    if i == j:
                        block = jnp.where(low_left(), corner_parts[i], block)
                    part[c][h][:, side, n] = block.reshape(16, 8, T)

    order = (2, 1, 3)

    def send_x(c):
        for half in range(2):
            for k in order:
                x_copy(c, k, half).start()

    def half_sent(c):
        for k in order:
            x_copy(c, k, 0).wait_send()

    def arrive(c):
        own[c].wait()
        for half in range(2):
            for k in order:
                x_copy(c, k, half).wait_recv()
        for h in range(2):
            for side in range(2):
                gram(c, h, side)
            z_copy(c, h).start()

    def pass_on(c, h):
        z_copy(c, h).wait_recv()
        part[c][h][pl.ds(b0 * 8, 8)] += r1[c][h][...]
        for to in places:
            w_copy(c, h, to).start()
        r3[c][h][x * 2 + b1] = part[c][h][piece]

    def settle(c, h):
        for to in places:
            w_landed(c, h, to).wait_recv()
        for i in range(4):
            xt[h][4 * i + 2 * c:4 * i + 2 * c + 2] = r3[c][h][2 * i] + r3[c][h][2 * i + 1]

    @pl.when(core == 1)
    def _():
        pl.semaphore_wait(turn, 1)

    send_x(0)
    for g in range(16):
        pick = jnp.int32(0)
        for j in range(16):
            pick = jnp.where(lax.shift_right_logical(table[f, j], 4) == g, j, pick)
        items[g] = pick
    half_sent(0)
    send_x(1)
    lax.fori_loop(0, 16, find_column, 0)
    for axis, peers in enumerate((along_z, along_y, [across])):
        for peer in peers:
            pl.semaphore_signal(ready.at[axis], inc=1, device_id=peer, device_id_type=MESH)
        pl.semaphore_wait(ready.at[axis], len(peers))

    arrive(0)
    half_sent(1)

    @pl.when(core == 0)
    def _():
        pl.semaphore_signal(turn, inc=1, device_id=partner, device_id_type=MESH)

    for h in range(2):
        pass_on(0, h)
    arrive(1)
    for h in range(2):
        settle(0, h)
    for h in range(2):
        pass_on(1, h)
    for h in range(2):
        settle(1, h)
        for g in others_f:
            fs[h][g] = xt[h][items[g]]
            a_copy(h, g).start()
        fr[h][f] = xt[h][items[f]]
    for h in range(2):
        for g in others_f:
            a_landed(h, g).wait_recv()
        for e in others_d:
            ds[h][e] = fr[h][columns[e]]
            b_copy(h, e).start()
        dr[h][piece] = fr[h][columns[d]]
    for h in range(2):
        for e in others_d:
            b_landed(h, e).wait_recv()
        out[h][...] = dr[h][...]

    for c in range(2):
        for k in order:
            x_copy(c, k, 1).wait_send()
        for h in range(2):
            z_copy(c, h).wait_send()
            for to in places:
                w_copy(c, h, to).wait_send()
    for h in range(2):
        for e in others_d:
            b_copy(h, e).wait_send()
        for g in others_f:
            a_copy(h, g).wait_send()


def routed(table, grads):
    tiles = [(len(blocks), 8, T) for blocks in PARTS]

    def buffers(*lead):
        return [pltpu.VMEM(lead + tile, jnp.float32) for tile in tiles]

    def semaphores(*shape):
        return [pltpu.SemaphoreType.DMA(shape)] * 2

    return pl.pallas_call(
        route,
        out_shape=tuple(jax.ShapeDtypeStruct((16,) + tile, jnp.float32) for tile in tiles),
        in_specs=[
            pl.BlockSpec(memory_space=pltpu.SMEM),
            pl.BlockSpec(memory_space=pltpu.HBM),
        ],
        out_specs=(pl.BlockSpec(memory_space=pltpu.VMEM),) * 2,
        scratch_shapes=[
            pltpu.VMEM((2, 4, B, B), jnp.bfloat16),
            *buffers(16, 2) * 2,
            *buffers(8, 2) * 2,
            *buffers(8, 2) * 2,
            *buffers(16) * 5,
            pltpu.SMEM((16,), jnp.int32),
            pltpu.SMEM((16,), jnp.int32),
            pltpu.SemaphoreType.DMA((2,)),
            *semaphores(2, 4, 2),
            *semaphores(2, 2),
            *semaphores(2, 2, 8),
            *semaphores(2, 16),
            *semaphores(2, 16),
            pltpu.SemaphoreType.REGULAR,
            pltpu.SemaphoreType.REGULAR((3,)),
        ],
        compiler_params=pltpu.CompilerParams(
            collective_id=0, has_side_effects=True, vmem_limit_bytes=52 * 1024 * 1024
        ),
        cost_estimate=pl.CostEstimate(flops=4 * 10**9, bytes_accessed=8 * 10**6, transcendentals=0),
        name="route",
    )(table, grads)


def split(a):
    high = a.astype(jnp.bfloat16)
    return high, (a - high.astype(jnp.float32)).astype(jnp.bfloat16)


def halves(matrix):
    return {place: split(quarter) for place, quarter in matrix.items()}


def product(a, b):
    out = {}
    for r, c in ((0, 0), (0, 1), (1, 1)):
        left, right = [], []
        for k in range(2):
            left += [a[r, k][0], a[r, k][0], a[r, k][1]]
            right += [b[k, c][0], b[k, c][1], b[k, c][0]]
        out[r, c] = jnp.dot(
            jnp.concatenate(left, axis=1), jnp.concatenate(right, axis=0), preferred_element_type=jnp.float32
        )
    out[1, 0] = out[0, 1].T
    return out


def newton(tri0, tri1, old, stats, roots):
    def blend(i, j, block):
        rows, cols = slice(i * T, (i + 1) * T), slice(j * T, (j + 1) * T)
        stats[rows, cols] = BETA * old[rows, cols] + (1.0 - BETA) * block

    mask = low_left()
    kept = []
    for tri, n, (i, j) in [(tri, n, p) for tri, ps in zip((tri0, tri1), PARTS) for n, p in enumerate(ps)]:
        block = tri[:, n].reshape(T, T)
        if i == j:
            kept.append(block)
            blend(i, i, jnp.where(mask, block.T, block))
        else:
            blend(i, j, block)
            blend(j, i, block.T)
    first, second, third = kept
    left = lax.broadcasted_iota(jnp.int32, (T // 2, T), 1) < T // 2
    top = jnp.where(left, first[T // 2:], turned(second[T // 2:]))
    corner = jnp.concatenate([top, turned(third[T // 2:])], axis=0)
    blend(3, 3, jnp.where(mask, corner.T, corner))

    scale = 2.5 / jnp.sqrt(jnp.sum(stats[...] * stats[...], keepdims=True) + 1e-06)
    eye = lax.broadcasted_iota(jnp.int32, (H, H), 0) == lax.broadcasted_iota(jnp.int32, (H, H), 1)

    def factor_of(matrix):
        return {
            (r, c): (jnp.where(eye, 1.25, 0.0) if r == c else 0.0) - 0.25 * quarter
            for (r, c), quarter in matrix.items()
        }

    moving = {
        (r, c): scale * stats[r * H:(r + 1) * H, c * H:(c + 1) * H] for r in range(2) for c in range(2)
    }
    root = factor_of(moving)
    factor = halves(root)
    for sweep in range(1, ITERS):
        square = halves(product(factor, factor))
        fourth = halves(product(square, square))
        moving = product(fourth, halves(moving))
        factor = halves(factor_of(moving))
        root = product(halves(root), factor)
    post = jnp.sqrt(jnp.sqrt(scale))
    for (r, c), quarter in root.items():
        roots[r * H:(r + 1) * H, c * H:(c + 1) * H] = post * quarter


def finished(tri0, tri1, old):
    whole = pl.BlockSpec(memory_space=pltpu.VMEM)
    return pl.pallas_call(
        newton,
        out_shape=(jax.ShapeDtypeStruct((B, B), jnp.float32),) * 2,
        in_specs=[whole] * 3,
        out_specs=(whole, whole),
        compiler_params=pltpu.CompilerParams(vmem_limit_bytes=48 * 1024 * 1024),
        cost_estimate=pl.CostEstimate(flops=13 * 10**9, bytes_accessed=4 * 10**6, transcendentals=0),
        name="newton",
    )(tri0, tri1, old)


def local(gradients, old_stats, owner_table):
    tri0, tri1 = routed(owner_table, gradients[0])
    stats, roots = finished(tri0, tri1, old_stats[0, 0])
    return (stats[None, None], roots[None, None])


def solution(mesh):
    placed = (P("dp", "factor", None, None), P("dp", "factor", None, None), P())
    return jax.shard_map(
        local,
        mesh=mesh,
        in_specs=placed,
        out_specs=(P("dp", "factor", None, None), P("dp", "factor", None, None)),
        check_vma=False,
    )
```

```python
import jax
import jax.numpy as jnp
from jax import lax
from jax.experimental import pallas as pl
from jax.experimental.pallas import tpu as pltpu
from jax.sharding import PartitionSpec as P

ITERS = 5
BETA = 0.9
B = 512
T = 128
MESH = pl.DeviceIdType.MESH
PARTS = (((0, 2), (0, 3), (1, 2), (1, 3)), ((0, 1), (2, 3), (0, 0), (1, 1), (2, 2)))
QUADS = (((0, 1),), ((1, 1), (0, 0)))
H = 256


def low_left():
    rows = lax.broadcasted_iota(jnp.int32, (T, T), 0)
    cols = lax.broadcasted_iota(jnp.int32, (T, T), 1)
    return jnp.logical_and(rows >= T // 2, cols < T // 2)


def swapped(block):
    return jnp.concatenate([block[T // 2:], block[:T // 2]], axis=0)


def turned(block):
    return jnp.concatenate([block[:, T // 2:], block[:, :T // 2]], axis=1)


def route(table, grads, out0, out1, xg, *refs):
    pairs = [(refs[2 * i], refs[2 * i + 1]) for i in range(11)]
    part, r1, r3 = ([pairs[2 * i], pairs[2 * i + 1]] for i in range(3))
    xt, fs, fr, ds, dr = pairs[6:]
    items, columns, own_sem, xs, xr, zs, zr, ws, wr, as_, ar, bs, br, turn, ready = refs[22:]
    out = (out0, out1)
    d = lax.axis_index("dp")
    f = lax.axis_index("factor")
    x, zl = d // 4, d % 4
    zh, y, core = f // 8, (f // 2) % 4, f % 2
    q = zl + zh * (3 - 2 * zl)
    b0, b1 = q % 2, q // 2
    piece = b0 * 8 + b1 * 4 + x

    def dp_at(x_, q_, zh_):
        return x_ * 4 + q_ + zh_ * (3 - 2 * q_)

    def x_peer(k):
        return {"dp": dp_at((x + k) % 4, q, zh), "factor": f}

    def f_peer(g):
        return {"dp": dp_at(x, q, g // 8), "factor": g}

    def d_peer(e):
        return {"dp": e, "factor": f}

    partner = {"dp": d, "factor": f + 1 - 2 * core}
    along_z = [{"dp": dp_at(x, (q + k) % 4, zh), "factor": f} for k in range(1, 4)]
    along_y = [{"dp": d, "factor": zh * 8 + ((y + k) % 4) * 2 + core} for k in range(1, 4)]
    across = {"dp": dp_at(x, q, 1 - zh), "factor": (1 - zh) * 8 + y * 2 + core}
    barrier = pltpu.get_barrier_semaphore()
    for peer in [x_peer(k) for k in range(1, 4)] + [partner] + along_z + along_y + [across]:
        pl.semaphore_signal(barrier, inc=1, device_id=peer, device_id_type=MESH)
    own = [pltpu.make_async_copy(grads.at[2 * x + c], xg.at[c, 0], own_sem.at[c]) for c in range(2)]
    for copy in own:
        copy.start()

    others_d = [(d + k) % 16 for k in range(1, 16)]
    others_f = [(f + k) % 16 for k in range(1, 16)]

    def find_column(e, carry):
        def scan(c, found):
            for j in range(16):
                found = jnp.where(table[c, j] == f * 16 + e, c, found)
            return found
        columns[e] = lax.fori_loop(0, 16, scan, jnp.int32(0))
        return carry

    pl.semaphore_wait(barrier, 11)

    def x_copy(c, k, half):
        rows = pl.ds(half * H, H)
        return pltpu.make_async_remote_copy(
            src_ref=grads.at[2 * ((x + k) % 4) + c, rows], dst_ref=xg.at[c, k, rows],
            send_sem=xs.at[c, k, half], recv_sem=xr.at[c, k, half], device_id=x_peer(k), device_id_type=MESH)

    def z_copy(c, h):
        return pltpu.make_async_remote_copy(
            src_ref=part[c][h].at[pl.ds((1 - b0) * 8, 8)], dst_ref=r1[c][h],
            send_sem=zs.at[c, h], recv_sem=zr.at[c, h],
            device_id={"dp": dp_at(x, q + 1 - 2 * b0, zh), "factor": f}, device_id_type=MESH)

    places = [((x + k) % 4, up) for k in range(1, 4) for up in (1 - b1, b1)] + [(x, 1 - b1)]

    def w_copy(c, h, to):
        slot = to[0] * 2 + to[1]
        return pltpu.make_async_remote_copy(
            src_ref=part[c][h].at[b0 * 8 + to[1] * 4 + to[0]], dst_ref=r3[c][h].at[x * 2 + b1],
            send_sem=ws.at[c, h, slot], recv_sem=wr.at[c, h, x * 2 + b1],
            device_id={"dp": dp_at(to[0], b0 + 2 * to[1], zh), "factor": f}, device_id_type=MESH)

    def w_landed(c, h, to):
        slot = to[0] * 2 + to[1]
        return pltpu.make_async_remote_copy(
            src_ref=part[c][h].at[b0 * 8 + to[1] * 4 + to[0]], dst_ref=r3[c][h].at[slot],
            send_sem=ws.at[c, h, slot], recv_sem=wr.at[c, h, slot],
            device_id={"dp": dp_at(to[0], b0 + 2 * to[1], zh), "factor": f}, device_id_type=MESH)

    def piece_of(e):
        e_x, e_zl = e // 4, e % 4
        e_q = e_zl + zh * (3 - 2 * e_zl)
        return (e_q % 2) * 8 + (e_q // 2) * 4 + e_x

    def a_copy(h, g):
        return pltpu.make_async_remote_copy(
            src_ref=fs[h].at[g], dst_ref=fr[h].at[f], send_sem=as_.at[h, g], recv_sem=ar.at[h, f],
            device_id=f_peer(g), device_id_type=MESH)

    def a_landed(h, g):
        return pltpu.make_async_remote_copy(
            src_ref=fs[h].at[g], dst_ref=fr[h].at[g], send_sem=as_.at[h, g], recv_sem=ar.at[h, g],
            device_id=f_peer(g), device_id_type=MESH)

    def b_copy(h, e):
        return pltpu.make_async_remote_copy(
            src_ref=ds[h].at[e], dst_ref=dr[h].at[piece], send_sem=bs.at[h, e], recv_sem=br.at[h, piece],
            device_id=d_peer(e), device_id_type=MESH)

    def b_landed(h, e):
        e_piece = piece_of(e)
        return pltpu.make_async_remote_copy(
            src_ref=ds[h].at[e], dst_ref=dr[h].at[e_piece], send_sem=bs.at[h, e], recv_sem=br.at[h, e_piece],
            device_id=d_peer(e), device_id_type=MESH)

    def gram(c, h, side):
        corner = None
        for row, col in QUADS[h]:
            total = None
            for k in range(4):
                if side == 0:
                    left = xg[c, k, row * H:(row + 1) * H, :]
                    right = xg[c, k, col * H:(col + 1) * H, :]
                    dims = (((1,), (1,)), ((), ()))
                else:
                    left = xg[c, k, :, row * H:(row + 1) * H]
                    right = xg[c, k, :, col * H:(col + 1) * H]
                    dims = (((0,), (0,)), ((), ()))
                term = lax.dot_general(left, right, dims, preferred_element_type=jnp.float32)
                total = term if total is None else total + term
            if (row, col) == (1, 1):
                corner = total[T:, T:]
                shifted = swapped(corner)
                corner_parts = (shifted, turned(shifted), turned(corner))
            for n, (i, j) in enumerate(PARTS[h]):
                if i // 2 == row and j // 2 == col:
                    i0, j0 = (i % 2) * T, (j % 2) * T
                    block = total[i0:i0 + T, j0:j0 + T]
                    if i == j:
                        block = jnp.where(low_left(), corner_parts[i], block)
                    part[c][h][:, side, n] = block.reshape(16, 8, T)

    order = (2, 1, 3)

    def send_x(c):
        for half in range(2):
            for k in order:
                x_copy(c, k, half).start()

    def half_sent(c):
        for k in order:
            x_copy(c, k, 0).wait_send()

    def arrive(c):
        own[c].wait()
        for half in range(2):
            for k in order:
                x_copy(c, k, half).wait_recv()
        for h in range(2):
            for side in range(2):
                gram(c, h, side)
            z_copy(c, h).start()

    def pass_on(c, h):
        z_copy(c, h).wait_recv()
        part[c][h][pl.ds(b0 * 8, 8)] += r1[c][h][...]
        for to in places:
            w_copy(c, h, to).start()
        r3[c][h][x * 2 + b1] = part[c][h][piece]

    def settle(c, h):
        for to in places:
            w_landed(c, h, to).wait_recv()
        for i in range(4):
            xt[h][4 * i + 2 * c:4 * i + 2 * c + 2] = r3[c][h][2 * i] + r3[c][h][2 * i + 1]

    @pl.when(core == 1)
    def _():
        pl.semaphore_wait(turn, 1)

    send_x(0)
    for g in range(16):
        pick = jnp.int32(0)
        for j in range(16):
            pick = jnp.where(lax.shift_right_logical(table[f, j], 4) == g, j, pick)
        items[g] = pick
    half_sent(0)
    send_x(1)
    lax.fori_loop(0, 16, find_column, 0)
    for axis, peers in enumerate((along_z, along_y, [across])):
        for peer in peers:
            pl.semaphore_signal(ready.at[axis], inc=1, device_id=peer, device_id_type=MESH)
        pl.semaphore_wait(ready.at[axis], len(peers))

    arrive(0)
    half_sent(1)

    @pl.when(core == 0)
    def _():
        pl.semaphore_signal(turn, inc=1, device_id=partner, device_id_type=MESH)

    for h in range(2):
        pass_on(0, h)
    arrive(1)
    for h in range(2):
        pass_on(1, h)
    for h in range(2):
        settle(0, h)
        settle(1, h)
        for g in others_f:
            fs[h][g] = xt[h][items[g]]
            a_copy(h, g).start()
        fr[h][f] = xt[h][items[f]]
    for h in range(2):
        for g in others_f:
            a_landed(h, g).wait_recv()
        for e in others_d:
            ds[h][e] = fr[h][columns[e]]
            b_copy(h, e).start()
        dr[h][piece] = fr[h][columns[d]]
    for h in range(2):
        for e in others_d:
            b_landed(h, e).wait_recv()
        out[h][...] = dr[h][...]

    for c in range(2):
        for k in order:
            x_copy(c, k, 1).wait_send()
        for h in range(2):
            z_copy(c, h).wait_send()
            for to in places:
                w_copy(c, h, to).wait_send()
    for h in range(2):
        for e in others_d:
            b_copy(h, e).wait_send()
        for g in others_f:
            a_copy(h, g).wait_send()


def routed(table, grads):
    tiles = [(len(blocks), 8, T) for blocks in PARTS]

    def buffers(*lead):
        return [pltpu.VMEM(lead + tile, jnp.float32) for tile in tiles]

    def semaphores(*shape):
        return [pltpu.SemaphoreType.DMA(shape)] * 2

    return pl.pallas_call(
        route,
        out_shape=tuple(jax.ShapeDtypeStruct((16,) + tile, jnp.float32) for tile in tiles),
        in_specs=[
            pl.BlockSpec(memory_space=pltpu.SMEM),
            pl.BlockSpec(memory_space=pltpu.HBM),
        ],
        out_specs=(pl.BlockSpec(memory_space=pltpu.VMEM),) * 2,
        scratch_shapes=[
            pltpu.VMEM((2, 4, B, B), jnp.bfloat16),
            *buffers(16, 2) * 2,
            *buffers(8, 2) * 2,
            *buffers(8, 2) * 2,
            *buffers(16) * 5,
            pltpu.SMEM((16,), jnp.int32),
            pltpu.SMEM((16,), jnp.int32),
            pltpu.SemaphoreType.DMA((2,)),
            *semaphores(2, 4, 2),
            *semaphores(2, 2),
            *semaphores(2, 2, 8),
            *semaphores(2, 16),
            *semaphores(2, 16),
            pltpu.SemaphoreType.REGULAR,
            pltpu.SemaphoreType.REGULAR((3,)),
        ],
        compiler_params=pltpu.CompilerParams(
            collective_id=0, has_side_effects=True, vmem_limit_bytes=52 * 1024 * 1024
        ),
        cost_estimate=pl.CostEstimate(flops=4 * 10**9, bytes_accessed=8 * 10**6, transcendentals=0),
        name="route",
    )(table, grads)


def split(a):
    high = a.astype(jnp.bfloat16)
    return high, (a - high.astype(jnp.float32)).astype(jnp.bfloat16)


def halves(matrix):
    return {place: split(quarter) for place, quarter in matrix.items()}


def product(a, b):
    out = {}
    for r, c in ((0, 0), (0, 1), (1, 1)):
        left, right = [], []
        for k in range(2):
            left += [a[r, k][0], a[r, k][0], a[r, k][1]]
            right += [b[k, c][0], b[k, c][1], b[k, c][0]]
        out[r, c] = jnp.dot(
            jnp.concatenate(left, axis=1), jnp.concatenate(right, axis=0), preferred_element_type=jnp.float32
        )
    out[1, 0] = out[0, 1].T
    return out


def newton(tri0, tri1, old, stats, roots):
    def blend(i, j, block):
        rows, cols = slice(i * T, (i + 1) * T), slice(j * T, (j + 1) * T)
        stats[rows, cols] = BETA * old[rows, cols] + (1.0 - BETA) * block

    mask = low_left()
    kept = []
    for tri, n, (i, j) in [(tri, n, p) for tri, ps in zip((tri0, tri1), PARTS) for n, p in enumerate(ps)]:
        block = tri[:, n].reshape(T, T)
        if i == j:
            kept.append(block)
            blend(i, i, jnp.where(mask, block.T, block))
        else:
            blend(i, j, block)
            blend(j, i, block.T)
    first, second, third = kept
    left = lax.broadcasted_iota(jnp.int32, (T // 2, T), 1) < T // 2
    top = jnp.where(left, first[T // 2:], turned(second[T // 2:]))
    corner = jnp.concatenate([top, turned(third[T // 2:])], axis=0)
    blend(3, 3, jnp.where(mask, corner.T, corner))

    scale = 2.5 / jnp.sqrt(jnp.sum(stats[...] * stats[...], keepdims=True) + 1e-06)
    eye = lax.broadcasted_iota(jnp.int32, (H, H), 0) == lax.broadcasted_iota(jnp.int32, (H, H), 1)

    def factor_of(matrix):
        return {
            (r, c): (jnp.where(eye, 1.25, 0.0) if r == c else 0.0) - 0.25 * quarter
            for (r, c), quarter in matrix.items()
        }

    moving = {
        (r, c): scale * stats[r * H:(r + 1) * H, c * H:(c + 1) * H] for r in range(2) for c in range(2)
    }
    root = factor_of(moving)
    factor = halves(root)
    for sweep in range(1, ITERS):
        square = halves(product(factor, factor))
        fourth = halves(product(square, square))
        moving = product(fourth, halves(moving))
        factor = halves(factor_of(moving))
        root = product(halves(root), factor)
    post = jnp.sqrt(jnp.sqrt(scale))
    for (r, c), quarter in root.items():
        roots[r * H:(r + 1) * H, c * H:(c + 1) * H] = post * quarter


def finished(tri0, tri1, old):
    whole = pl.BlockSpec(memory_space=pltpu.VMEM)
    return pl.pallas_call(
        newton,
        out_shape=(jax.ShapeDtypeStruct((B, B), jnp.float32),) * 2,
        in_specs=[whole] * 3,
        out_specs=(whole, whole),
        compiler_params=pltpu.CompilerParams(vmem_limit_bytes=48 * 1024 * 1024),
        cost_estimate=pl.CostEstimate(flops=13 * 10**9, bytes_accessed=4 * 10**6, transcendentals=0),
        name="newton",
    )(tri0, tri1, old)


def local(gradients, old_stats, owner_table):
    tri0, tri1 = routed(owner_table, gradients[0])
    stats, roots = finished(tri0, tri1, old_stats[0, 0])
    return (stats[None, None], roots[None, None])


def solution(mesh):
    placed = (P("dp", "factor", None, None), P("dp", "factor", None, None), P())
    return jax.shard_map(
        local,
        mesh=mesh,
        in_specs=placed,
        out_specs=(P("dp", "factor", None, None), P("dp", "factor", None, None)),
        check_vma=False,
    )
```

```python
import jax
import jax.numpy as jnp
from jax import lax
from jax.experimental import pallas as pl
from jax.experimental.pallas import tpu as pltpu
from jax.sharding import PartitionSpec as P

ITERS = 5
BETA = 0.9
B = 512
T = 128
MESH = pl.DeviceIdType.MESH
PARTS = (((0, 2), (0, 3), (1, 2), (1, 3)), ((0, 1), (2, 3), (0, 0), (1, 1), (2, 2)))
QUADS = (((0, 1),), ((1, 1), (0, 0)))
H = 256


def low_left():
    rows = lax.broadcasted_iota(jnp.int32, (T, T), 0)
    cols = lax.broadcasted_iota(jnp.int32, (T, T), 1)
    return jnp.logical_and(rows >= T // 2, cols < T // 2)


def swapped(block):
    return jnp.concatenate([block[T // 2:], block[:T // 2]], axis=0)


def turned(block):
    return jnp.concatenate([block[:, T // 2:], block[:, :T // 2]], axis=1)


def route(table, grads, out0, out1, xg, *refs):
    pairs = [(refs[2 * i], refs[2 * i + 1]) for i in range(11)]
    part, r1, r3 = ([pairs[2 * i], pairs[2 * i + 1]] for i in range(3))
    xt, fs, fr, ds, dr = pairs[6:]
    items, columns, own_sem, xs, xr, zs, zr, ws, wr, as_, ar, bs, br, turn, ready = refs[22:]
    out = (out0, out1)
    d = lax.axis_index("dp")
    f = lax.axis_index("factor")
    x, zl = d // 4, d % 4
    zh, y, core = f // 8, (f // 2) % 4, f % 2
    q = zl + zh * (3 - 2 * zl)
    b0, b1 = q % 2, q // 2
    piece = b0 * 8 + b1 * 4 + x

    def dp_at(x_, q_, zh_):
        return x_ * 4 + q_ + zh_ * (3 - 2 * q_)

    def x_peer(k):
        return {"dp": dp_at((x + k) % 4, q, zh), "factor": f}

    def f_peer(g):
        return {"dp": dp_at(x, q, g // 8), "factor": g}

    def d_peer(e):
        return {"dp": e, "factor": f}

    partner = {"dp": d, "factor": f + 1 - 2 * core}
    along_z = [{"dp": dp_at(x, (q + k) % 4, zh), "factor": f} for k in range(1, 4)]
    along_y = [{"dp": d, "factor": zh * 8 + ((y + k) % 4) * 2 + core} for k in range(1, 4)]
    across = {"dp": dp_at(x, q, 1 - zh), "factor": (1 - zh) * 8 + y * 2 + core}
    barrier = pltpu.get_barrier_semaphore()
    for peer in [x_peer(k) for k in range(1, 4)] + [partner] + along_z + along_y + [across]:
        pl.semaphore_signal(barrier, inc=1, device_id=peer, device_id_type=MESH)
    own = [pltpu.make_async_copy(grads.at[2 * x + c], xg.at[c, 0], own_sem.at[c]) for c in range(2)]
    for copy in own:
        copy.start()

    others_d = [(d + k) % 16 for k in range(1, 16)]
    others_f = [(f + k) % 16 for k in range(1, 16)]

    def find_column(e, carry):
        def scan(c, found):
            for j in range(16):
                found = jnp.where(table[c, j] == f * 16 + e, c, found)
            return found
        columns[e] = lax.fori_loop(0, 16, scan, jnp.int32(0))
        return carry

    pl.semaphore_wait(barrier, 11)

    def x_copy(c, k, half):
        rows = pl.ds(0, 384) if half == 0 else pl.ds(384, 128)
        return pltpu.make_async_remote_copy(
            src_ref=grads.at[2 * ((x + k) % 4) + c, rows], dst_ref=xg.at[c, k, rows],
            send_sem=xs.at[c, k, half], recv_sem=xr.at[c, k, half], device_id=x_peer(k), device_id_type=MESH)

    def z_copy(c, h):
        return pltpu.make_async_remote_copy(
            src_ref=part[c][h].at[pl.ds((1 - b0) * 8, 8)], dst_ref=r1[c][h],
            send_sem=zs.at[c, h], recv_sem=zr.at[c, h],
            device_id={"dp": dp_at(x, q + 1 - 2 * b0, zh), "factor": f}, device_id_type=MESH)

    places = [((x + k) % 4, up) for k in range(1, 4) for up in (1 - b1, b1)] + [(x, 1 - b1)]

    def w_copy(c, h, to):
        slot = to[0] * 2 + to[1]
        return pltpu.make_async_remote_copy(
            src_ref=part[c][h].at[b0 * 8 + to[1] * 4 + to[0]], dst_ref=r3[c][h].at[x * 2 + b1],
            send_sem=ws.at[c, h, slot], recv_sem=wr.at[c, h, x * 2 + b1],
            device_id={"dp": dp_at(to[0], b0 + 2 * to[1], zh), "factor": f}, device_id_type=MESH)

    def w_landed(c, h, to):
        slot = to[0] * 2 + to[1]
        return pltpu.make_async_remote_copy(
            src_ref=part[c][h].at[b0 * 8 + to[1] * 4 + to[0]], dst_ref=r3[c][h].at[slot],
            send_sem=ws.at[c, h, slot], recv_sem=wr.at[c, h, slot],
            device_id={"dp": dp_at(to[0], b0 + 2 * to[1], zh), "factor": f}, device_id_type=MESH)

    def piece_of(e):
        e_x, e_zl = e // 4, e % 4
        e_q = e_zl + zh * (3 - 2 * e_zl)
        return (e_q % 2) * 8 + (e_q // 2) * 4 + e_x

    def a_copy(h, g):
        return pltpu.make_async_remote_copy(
            src_ref=fs[h].at[g], dst_ref=fr[h].at[f], send_sem=as_.at[h, g], recv_sem=ar.at[h, f],
            device_id=f_peer(g), device_id_type=MESH)

    def a_landed(h, g):
        return pltpu.make_async_remote_copy(
            src_ref=fs[h].at[g], dst_ref=fr[h].at[g], send_sem=as_.at[h, g], recv_sem=ar.at[h, g],
            device_id=f_peer(g), device_id_type=MESH)

    def b_copy(h, e):
        return pltpu.make_async_remote_copy(
            src_ref=ds[h].at[e], dst_ref=dr[h].at[piece], send_sem=bs.at[h, e], recv_sem=br.at[h, piece],
            device_id=d_peer(e), device_id_type=MESH)

    def b_landed(h, e):
        e_piece = piece_of(e)
        return pltpu.make_async_remote_copy(
            src_ref=ds[h].at[e], dst_ref=dr[h].at[e_piece], send_sem=bs.at[h, e], recv_sem=br.at[h, e_piece],
            device_id=d_peer(e), device_id_type=MESH)

    def gram(c, h, side):
        corner = None
        for row, col in QUADS[h]:
            total = None
            for k in range(4):
                if side == 0:
                    left = xg[c, k, row * H:(row + 1) * H, :]
                    right = xg[c, k, col * H:(col + 1) * H, :]
                    dims = (((1,), (1,)), ((), ()))
                else:
                    left = xg[c, k, :, row * H:(row + 1) * H]
                    right = xg[c, k, :, col * H:(col + 1) * H]
                    dims = (((0,), (0,)), ((), ()))
                term = lax.dot_general(left, right, dims, preferred_element_type=jnp.float32)
                total = term if total is None else total + term
            if (row, col) == (1, 1):
                corner = total[T:, T:]
                shifted = swapped(corner)
                corner_parts = (shifted, turned(shifted), turned(corner))
            for n, (i, j) in enumerate(PARTS[h]):
                if i // 2 == row and j // 2 == col:
                    i0, j0 = (i % 2) * T, (j % 2) * T
                    block = total[i0:i0 + T, j0:j0 + T]
                    if i == j:
                        block = jnp.where(low_left(), corner_parts[i], block)
                    part[c][h][:, side, n] = block.reshape(16, 8, T)

    order = (2, 1, 3)

    def send_x(c):
        for half in range(2):
            for k in order:
                x_copy(c, k, half).start()

    def half_sent(c):
        for k in order:
            x_copy(c, k, 0).wait_send()

    def arrive(c):
        own[c].wait()
        for half in range(2):
            for k in order:
                x_copy(c, k, half).wait_recv()
        for h in range(2):
            for side in range(2):
                gram(c, h, side)
            z_copy(c, h).start()

    def pass_on(c, h):
        z_copy(c, h).wait_recv()
        part[c][h][pl.ds(b0 * 8, 8)] += r1[c][h][...]
        for to in places:
            w_copy(c, h, to).start()
        r3[c][h][x * 2 + b1] = part[c][h][piece]

    def settle(c, h):
        for to in places:
            w_landed(c, h, to).wait_recv()
        for i in range(4):
            xt[h][4 * i + 2 * c:4 * i + 2 * c + 2] = r3[c][h][2 * i] + r3[c][h][2 * i + 1]

    @pl.when(core == 1)
    def _():
        pl.semaphore_wait(turn, 1)

    send_x(0)
    for g in range(16):
        pick = jnp.int32(0)
        for j in range(16):
            pick = jnp.where(lax.shift_right_logical(table[f, j], 4) == g, j, pick)
        items[g] = pick
    half_sent(0)
    pl.semaphore_signal(turn, inc=1, device_id=partner, device_id_type=MESH)
    lax.fori_loop(0, 16, find_column, 0)
    for axis, peers in enumerate((along_z, along_y, [across])):
        for peer in peers:
            pl.semaphore_signal(ready.at[axis], inc=1, device_id=peer, device_id_type=MESH)
        pl.semaphore_wait(ready.at[axis], len(peers))

    arrive(0)
    pl.semaphore_wait(turn, 1)
    send_x(1)
    for h in range(2):
        pass_on(0, h)
    half_sent(1)

    @pl.when(core == 0)
    def _():
        pl.semaphore_signal(turn, inc=1, device_id=partner, device_id_type=MESH)

    arrive(1)
    for h in range(2):
        pass_on(1, h)
    for h in range(2):
        settle(0, h)
        settle(1, h)
        for g in others_f:
            fs[h][g] = xt[h][items[g]]
            a_copy(h, g).start()
        fr[h][f] = xt[h][items[f]]
    for h in range(2):
        for g in others_f:
            a_landed(h, g).wait_recv()
        for e in others_d:
            ds[h][e] = fr[h][columns[e]]
            b_copy(h, e).start()
        dr[h][piece] = fr[h][columns[d]]
    for h in range(2):
        for e in others_d:
            b_landed(h, e).wait_recv()
        out[h][...] = dr[h][...]

    for c in range(2):
        for k in order:
            x_copy(c, k, 1).wait_send()
        for h in range(2):
            z_copy(c, h).wait_send()
            for to in places:
                w_copy(c, h, to).wait_send()
    for h in range(2):
        for e in others_d:
            b_copy(h, e).wait_send()
        for g in others_f:
            a_copy(h, g).wait_send()


def routed(table, grads):
    tiles = [(len(blocks), 8, T) for blocks in PARTS]

    def buffers(*lead):
        return [pltpu.VMEM(lead + tile, jnp.float32) for tile in tiles]

    def semaphores(*shape):
        return [pltpu.SemaphoreType.DMA(shape)] * 2

    return pl.pallas_call(
        route,
        out_shape=tuple(jax.ShapeDtypeStruct((16,) + tile, jnp.float32) for tile in tiles),
        in_specs=[
            pl.BlockSpec(memory_space=pltpu.SMEM),
            pl.BlockSpec(memory_space=pltpu.HBM),
        ],
        out_specs=(pl.BlockSpec(memory_space=pltpu.VMEM),) * 2,
        scratch_shapes=[
            pltpu.VMEM((2, 4, B, B), jnp.bfloat16),
            *buffers(16, 2) * 2,
            *buffers(8, 2) * 2,
            *buffers(8, 2) * 2,
            *buffers(16) * 5,
            pltpu.SMEM((16,), jnp.int32),
            pltpu.SMEM((16,), jnp.int32),
            pltpu.SemaphoreType.DMA((2,)),
            *semaphores(2, 4, 2),
            *semaphores(2, 2),
            *semaphores(2, 2, 8),
            *semaphores(2, 16),
            *semaphores(2, 16),
            pltpu.SemaphoreType.REGULAR,
            pltpu.SemaphoreType.REGULAR((3,)),
        ],
        compiler_params=pltpu.CompilerParams(
            collective_id=0, has_side_effects=True, vmem_limit_bytes=52 * 1024 * 1024
        ),
        cost_estimate=pl.CostEstimate(flops=4 * 10**9, bytes_accessed=8 * 10**6, transcendentals=0),
        name="route",
    )(table, grads)


def split(a):
    high = a.astype(jnp.bfloat16)
    return high, (a - high.astype(jnp.float32)).astype(jnp.bfloat16)


def halves(matrix):
    return {place: split(quarter) for place, quarter in matrix.items()}


def product(a, b):
    out = {}
    for r, c in ((0, 0), (0, 1), (1, 1)):
        left, right = [], []
        for k in range(2):
            left += [a[r, k][0], a[r, k][0], a[r, k][1]]
            right += [b[k, c][0], b[k, c][1], b[k, c][0]]
        out[r, c] = jnp.dot(
            jnp.concatenate(left, axis=1), jnp.concatenate(right, axis=0), preferred_element_type=jnp.float32
        )
    out[1, 0] = out[0, 1].T
    return out


def newton(tri0, tri1, old, stats, roots):
    def blend(i, j, block):
        rows, cols = slice(i * T, (i + 1) * T), slice(j * T, (j + 1) * T)
        stats[rows, cols] = BETA * old[rows, cols] + (1.0 - BETA) * block

    mask = low_left()
    kept = []
    for tri, n, (i, j) in [(tri, n, p) for tri, ps in zip((tri0, tri1), PARTS) for n, p in enumerate(ps)]:
        block = tri[:, n].reshape(T, T)
        if i == j:
            kept.append(block)
            blend(i, i, jnp.where(mask, block.T, block))
        else:
            blend(i, j, block)
            blend(j, i, block.T)
    first, second, third = kept
    left = lax.broadcasted_iota(jnp.int32, (T // 2, T), 1) < T // 2
    top = jnp.where(left, first[T // 2:], turned(second[T // 2:]))
    corner = jnp.concatenate([top, turned(third[T // 2:])], axis=0)
    blend(3, 3, jnp.where(mask, corner.T, corner))

    scale = 2.5 / jnp.sqrt(jnp.sum(stats[...] * stats[...], keepdims=True) + 1e-06)
    eye = lax.broadcasted_iota(jnp.int32, (H, H), 0) == lax.broadcasted_iota(jnp.int32, (H, H), 1)

    def factor_of(matrix):
        return {
            (r, c): (jnp.where(eye, 1.25, 0.0) if r == c else 0.0) - 0.25 * quarter
            for (r, c), quarter in matrix.items()
        }

    moving = {
        (r, c): scale * stats[r * H:(r + 1) * H, c * H:(c + 1) * H] for r in range(2) for c in range(2)
    }
    root = factor_of(moving)
    factor = halves(root)
    for sweep in range(1, ITERS):
        square = halves(product(factor, factor))
        fourth = halves(product(square, square))
        moving = product(fourth, halves(moving))
        factor = halves(factor_of(moving))
        root = product(halves(root), factor)
    post = jnp.sqrt(jnp.sqrt(scale))
    for (r, c), quarter in root.items():
        roots[r * H:(r + 1) * H, c * H:(c + 1) * H] = post * quarter


def finished(tri0, tri1, old):
    whole = pl.BlockSpec(memory_space=pltpu.VMEM)
    return pl.pallas_call(
        newton,
        out_shape=(jax.ShapeDtypeStruct((B, B), jnp.float32),) * 2,
        in_specs=[whole] * 3,
        out_specs=(whole, whole),
        compiler_params=pltpu.CompilerParams(vmem_limit_bytes=48 * 1024 * 1024),
        cost_estimate=pl.CostEstimate(flops=13 * 10**9, bytes_accessed=4 * 10**6, transcendentals=0),
        name="newton",
    )(tri0, tri1, old)


def local(gradients, old_stats, owner_table):
    tri0, tri1 = routed(owner_table, gradients[0])
    stats, roots = finished(tri0, tri1, old_stats[0, 0])
    return (stats[None, None], roots[None, None])


def solution(mesh):
    placed = (P("dp", "factor", None, None), P("dp", "factor", None, None), P())
    return jax.shard_map(
        local,
        mesh=mesh,
        in_specs=placed,
        out_specs=(P("dp", "factor", None, None), P("dp", "factor", None, None)),
        check_vma=False,
    )
```

```python
import jax
import jax.numpy as jnp
from jax import lax
from jax.experimental import pallas as pl
from jax.experimental.pallas import tpu as pltpu
from jax.sharding import PartitionSpec as P

ITERS = 5
BETA = 0.9
B = 512
T = 128
MESH = pl.DeviceIdType.MESH
PARTS = (((0, 2), (0, 3), (1, 2), (1, 3)), ((0, 1), (2, 3), (0, 0), (1, 1), (2, 2)))
QUADS = (((0, 1),), ((1, 1), (0, 0)))
H = 256


def low_left():
    rows = lax.broadcasted_iota(jnp.int32, (T, T), 0)
    cols = lax.broadcasted_iota(jnp.int32, (T, T), 1)
    return jnp.logical_and(rows >= T // 2, cols < T // 2)


def swapped(block):
    return jnp.concatenate([block[T // 2:], block[:T // 2]], axis=0)


def turned(block):
    return jnp.concatenate([block[:, T // 2:], block[:, :T // 2]], axis=1)


def route(table, grads, out0, out1, xg, *refs):
    pairs = [(refs[2 * i], refs[2 * i + 1]) for i in range(11)]
    part, r1, r3 = ([pairs[2 * i], pairs[2 * i + 1]] for i in range(3))
    xt, fs, fr, ds, dr = pairs[6:]
    items, columns, own_sem, xs, xr, zs, zr, ws, wr, as_, ar, bs, br, turn, ready = refs[22:]
    out = (out0, out1)
    d = lax.axis_index("dp")
    f = lax.axis_index("factor")
    x, zl = d // 4, d % 4
    zh, y, core = f // 8, (f // 2) % 4, f % 2
    q = zl + zh * (3 - 2 * zl)
    b0, b1 = q % 2, q // 2
    piece = b0 * 8 + b1 * 4 + x

    def dp_at(x_, q_, zh_):
        return x_ * 4 + q_ + zh_ * (3 - 2 * q_)

    def x_peer(k):
        return {"dp": dp_at((x + k) % 4, q, zh), "factor": f}

    def f_peer(g):
        return {"dp": dp_at(x, q, g // 8), "factor": g}

    def d_peer(e):
        return {"dp": e, "factor": f}

    partner = {"dp": d, "factor": f + 1 - 2 * core}
    along_z = [{"dp": dp_at(x, (q + k) % 4, zh), "factor": f} for k in range(1, 4)]
    along_y = [{"dp": d, "factor": zh * 8 + ((y + k) % 4) * 2 + core} for k in range(1, 4)]
    across = {"dp": dp_at(x, q, 1 - zh), "factor": (1 - zh) * 8 + y * 2 + core}
    barrier = pltpu.get_barrier_semaphore()
    for peer in [x_peer(k) for k in range(1, 4)] + [partner] + along_z + along_y + [across]:
        pl.semaphore_signal(barrier, inc=1, device_id=peer, device_id_type=MESH)
    own = [pltpu.make_async_copy(grads.at[2 * x + c], xg.at[c, 0], own_sem.at[c]) for c in range(2)]
    for copy in own:
        copy.start()

    others_d = [(d + k) % 16 for k in range(1, 16)]
    others_f = [(f + k) % 16 for k in range(1, 16)]

    def find_column(e, carry):
        def scan(c, found):
            for j in range(16):
                found = jnp.where(table[c, j] == f * 16 + e, c, found)
            return found
        columns[e] = lax.fori_loop(0, 16, scan, jnp.int32(0))
        return carry

    pl.semaphore_wait(barrier, 11)

    def x_copy(c, k, half):
        rows = pl.ds(half * H, H)
        return pltpu.make_async_remote_copy(
            src_ref=grads.at[2 * ((x + k) % 4) + c, rows], dst_ref=xg.at[c, k, rows],
            send_sem=xs.at[c, k, half], recv_sem=xr.at[c, k, half], device_id=x_peer(k), device_id_type=MESH)

    def z_copy(c, h):
        return pltpu.make_async_remote_copy(
            src_ref=part[c][h].at[pl.ds((1 - b0) * 8, 8)], dst_ref=r1[c][h],
            send_sem=zs.at[c, h], recv_sem=zr.at[c, h],
            device_id={"dp": dp_at(x, q + 1 - 2 * b0, zh), "factor": f}, device_id_type=MESH)

    places = [((x + k) % 4, up) for k in range(1, 4) for up in (1 - b1, b1)] + [(x, 1 - b1)]

    def w_copy(c, h, to):
        slot = to[0] * 2 + to[1]
        return pltpu.make_async_remote_copy(
            src_ref=part[c][h].at[b0 * 8 + to[1] * 4 + to[0]], dst_ref=r3[c][h].at[x * 2 + b1],
            send_sem=ws.at[c, h, slot], recv_sem=wr.at[c, h, x * 2 + b1],
            device_id={"dp": dp_at(to[0], b0 + 2 * to[1], zh), "factor": f}, device_id_type=MESH)

    def w_landed(c, h, to):
        slot = to[0] * 2 + to[1]
        return pltpu.make_async_remote_copy(
            src_ref=part[c][h].at[b0 * 8 + to[1] * 4 + to[0]], dst_ref=r3[c][h].at[slot],
            send_sem=ws.at[c, h, slot], recv_sem=wr.at[c, h, slot],
            device_id={"dp": dp_at(to[0], b0 + 2 * to[1], zh), "factor": f}, device_id_type=MESH)

    def piece_of(e):
        e_x, e_zl = e // 4, e % 4
        e_q = e_zl + zh * (3 - 2 * e_zl)
        return (e_q % 2) * 8 + (e_q // 2) * 4 + e_x

    def a_copy(h, g):
        return pltpu.make_async_remote_copy(
            src_ref=fs[h].at[g], dst_ref=fr[h].at[f], send_sem=as_.at[h, g], recv_sem=ar.at[h, f],
            device_id=f_peer(g), device_id_type=MESH)

    def a_landed(h, g):
        return pltpu.make_async_remote_copy(
            src_ref=fs[h].at[g], dst_ref=fr[h].at[g], send_sem=as_.at[h, g], recv_sem=ar.at[h, g],
            device_id=f_peer(g), device_id_type=MESH)

    def b_copy(h, e):
        return pltpu.make_async_remote_copy(
            src_ref=ds[h].at[e], dst_ref=dr[h].at[piece], send_sem=bs.at[h, e], recv_sem=br.at[h, piece],
            device_id=d_peer(e), device_id_type=MESH)

    def b_landed(h, e):
        e_piece = piece_of(e)
        return pltpu.make_async_remote_copy(
            src_ref=ds[h].at[e], dst_ref=dr[h].at[e_piece], send_sem=bs.at[h, e], recv_sem=br.at[h, e_piece],
            device_id=d_peer(e), device_id_type=MESH)

    def gram(c, h, side):
        corner = None
        for row, col in QUADS[h]:
            total = None
            for k in range(4):
                if side == 0:
                    left = xg[c, k, row * H:(row + 1) * H, :]
                    right = xg[c, k, col * H:(col + 1) * H, :]
                    dims = (((1,), (1,)), ((), ()))
                else:
                    left = xg[c, k, :, row * H:(row + 1) * H]
                    right = xg[c, k, :, col * H:(col + 1) * H]
                    dims = (((0,), (0,)), ((), ()))
                term = lax.dot_general(left, right, dims, preferred_element_type=jnp.float32)
                total = term if total is None else total + term
            if (row, col) == (1, 1):
                corner = total[T:, T:]
                shifted = swapped(corner)
                corner_parts = (shifted, turned(shifted), turned(corner))
            for n, (i, j) in enumerate(PARTS[h]):
                if i // 2 == row and j // 2 == col:
                    i0, j0 = (i % 2) * T, (j % 2) * T
                    block = total[i0:i0 + T, j0:j0 + T]
                    if i == j:
                        block = jnp.where(low_left(), corner_parts[i], block)
                    part[c][h][:, side, n] = block.reshape(16, 8, T)

    order = (2, 1, 3)

    def send_x(c):
        for half in range(2):
            for k in order:
                x_copy(c, k, half).start()

    def half_sent(c):
        for k in order:
            x_copy(c, k, 0).wait_send()

    def arrive(c):
        own[c].wait()
        for half in range(2):
            for k in order:
                x_copy(c, k, half).wait_recv()
        for h in range(2):
            for side in range(2):
                gram(c, h, side)
            z_copy(c, h).start()

    def pass_on(c, h):
        z_copy(c, h).wait_recv()
        part[c][h][pl.ds(b0 * 8, 8)] += r1[c][h][...]
        for to in places:
            w_copy(c, h, to).start()
        r3[c][h][x * 2 + b1] = part[c][h][piece]

    def settle(c, h):
        for to in places:
            w_landed(c, h, to).wait_recv()
        for i in range(4):
            xt[h][4 * i + 2 * c:4 * i + 2 * c + 2] = r3[c][h][2 * i] + r3[c][h][2 * i + 1]

    @pl.when(core == 1)
    def _():
        pl.semaphore_wait(turn, 1)

    send_x(0)
    for g in range(16):
        pick = jnp.int32(0)
        for j in range(16):
            pick = jnp.where(lax.shift_right_logical(table[f, j], 4) == g, j, pick)
        items[g] = pick
    half_sent(0)
    for k in order:
        x_copy(0, k, 1).wait_send()
    send_x(1)
    lax.fori_loop(0, 16, find_column, 0)
    for axis, peers in enumerate((along_z, along_y, [across])):
        for peer in peers:
            pl.semaphore_signal(ready.at[axis], inc=1, device_id=peer, device_id_type=MESH)
        pl.semaphore_wait(ready.at[axis], len(peers))

    arrive(0)
    half_sent(1)

    @pl.when(core == 0)
    def _():
        pl.semaphore_signal(turn, inc=1, device_id=partner, device_id_type=MESH)

    for h in range(2):
        pass_on(0, h)
    arrive(1)
    for h in range(2):
        pass_on(1, h)
    for h in range(2):
        settle(0, h)
        settle(1, h)
        for g in others_f:
            fs[h][g] = xt[h][items[g]]
            a_copy(h, g).start()
        fr[h][f] = xt[h][items[f]]
    for h in range(2):
        for g in others_f:
            a_landed(h, g).wait_recv()
        for e in others_d:
            ds[h][e] = fr[h][columns[e]]
            b_copy(h, e).start()
        dr[h][piece] = fr[h][columns[d]]
    for h in range(2):
        for e in others_d:
            b_landed(h, e).wait_recv()
        out[h][...] = dr[h][...]

    for k in order:
        x_copy(1, k, 1).wait_send()
    for c in range(2):
        for h in range(2):
            z_copy(c, h).wait_send()
            for to in places:
                w_copy(c, h, to).wait_send()
    for h in range(2):
        for e in others_d:
            b_copy(h, e).wait_send()
        for g in others_f:
            a_copy(h, g).wait_send()


def routed(table, grads):
    tiles = [(len(blocks), 8, T) for blocks in PARTS]

    def buffers(*lead):
        return [pltpu.VMEM(lead + tile, jnp.float32) for tile in tiles]

    def semaphores(*shape):
        return [pltpu.SemaphoreType.DMA(shape)] * 2

    return pl.pallas_call(
        route,
        out_shape=tuple(jax.ShapeDtypeStruct((16,) + tile, jnp.float32) for tile in tiles),
        in_specs=[
            pl.BlockSpec(memory_space=pltpu.SMEM),
            pl.BlockSpec(memory_space=pltpu.HBM),
        ],
        out_specs=(pl.BlockSpec(memory_space=pltpu.VMEM),) * 2,
        scratch_shapes=[
            pltpu.VMEM((2, 4, B, B), jnp.bfloat16),
            *buffers(16, 2) * 2,
            *buffers(8, 2) * 2,
            *buffers(8, 2) * 2,
            *buffers(16) * 5,
            pltpu.SMEM((16,), jnp.int32),
            pltpu.SMEM((16,), jnp.int32),
            pltpu.SemaphoreType.DMA((2,)),
            *semaphores(2, 4, 2),
            *semaphores(2, 2),
            *semaphores(2, 2, 8),
            *semaphores(2, 16),
            *semaphores(2, 16),
            pltpu.SemaphoreType.REGULAR,
            pltpu.SemaphoreType.REGULAR((3,)),
        ],
        compiler_params=pltpu.CompilerParams(
            collective_id=0, has_side_effects=True, vmem_limit_bytes=52 * 1024 * 1024
        ),
        cost_estimate=pl.CostEstimate(flops=4 * 10**9, bytes_accessed=8 * 10**6, transcendentals=0),
        name="route",
    )(table, grads)


def split(a):
    high = a.astype(jnp.bfloat16)
    return high, (a - high.astype(jnp.float32)).astype(jnp.bfloat16)


def halves(matrix):
    return {place: split(quarter) for place, quarter in matrix.items()}


def product(a, b):
    out = {}
    for r, c in ((0, 0), (0, 1), (1, 1)):
        left, right = [], []
        for k in range(2):
            left += [a[r, k][0], a[r, k][0], a[r, k][1]]
            right += [b[k, c][0], b[k, c][1], b[k, c][0]]
        out[r, c] = jnp.dot(
            jnp.concatenate(left, axis=1), jnp.concatenate(right, axis=0), preferred_element_type=jnp.float32
        )
    out[1, 0] = out[0, 1].T
    return out


def newton(tri0, tri1, old, stats, roots):
    def blend(i, j, block):
        rows, cols = slice(i * T, (i + 1) * T), slice(j * T, (j + 1) * T)
        stats[rows, cols] = BETA * old[rows, cols] + (1.0 - BETA) * block

    mask = low_left()
    kept = []
    for tri, n, (i, j) in [(tri, n, p) for tri, ps in zip((tri0, tri1), PARTS) for n, p in enumerate(ps)]:
        block = tri[:, n].reshape(T, T)
        if i == j:
            kept.append(block)
            blend(i, i, jnp.where(mask, block.T, block))
        else:
            blend(i, j, block)
            blend(j, i, block.T)
    first, second, third = kept
    left = lax.broadcasted_iota(jnp.int32, (T // 2, T), 1) < T // 2
    top = jnp.where(left, first[T // 2:], turned(second[T // 2:]))
    corner = jnp.concatenate([top, turned(third[T // 2:])], axis=0)
    blend(3, 3, jnp.where(mask, corner.T, corner))

    scale = 2.5 / jnp.sqrt(jnp.sum(stats[...] * stats[...], keepdims=True) + 1e-06)
    eye = lax.broadcasted_iota(jnp.int32, (H, H), 0) == lax.broadcasted_iota(jnp.int32, (H, H), 1)

    def factor_of(matrix):
        return {
            (r, c): (jnp.where(eye, 1.25, 0.0) if r == c else 0.0) - 0.25 * quarter
            for (r, c), quarter in matrix.items()
        }

    moving = {
        (r, c): scale * stats[r * H:(r + 1) * H, c * H:(c + 1) * H] for r in range(2) for c in range(2)
    }
    root = factor_of(moving)
    factor = halves(root)
    for sweep in range(1, ITERS):
        square = halves(product(factor, factor))
        fourth = halves(product(square, square))
        moving = product(fourth, halves(moving))
        factor = halves(factor_of(moving))
        root = product(halves(root), factor)
    post = jnp.sqrt(jnp.sqrt(scale))
    for (r, c), quarter in root.items():
        roots[r * H:(r + 1) * H, c * H:(c + 1) * H] = post * quarter


def finished(tri0, tri1, old):
    whole = pl.BlockSpec(memory_space=pltpu.VMEM)
    return pl.pallas_call(
        newton,
        out_shape=(jax.ShapeDtypeStruct((B, B), jnp.float32),) * 2,
        in_specs=[whole] * 3,
        out_specs=(whole, whole),
        compiler_params=pltpu.CompilerParams(vmem_limit_bytes=48 * 1024 * 1024),
        cost_estimate=pl.CostEstimate(flops=13 * 10**9, bytes_accessed=4 * 10**6, transcendentals=0),
        name="newton",
    )(tri0, tri1, old)


def local(gradients, old_stats, owner_table):
    tri0, tri1 = routed(owner_table, gradients[0])
    stats, roots = finished(tri0, tri1, old_stats[0, 0])
    return (stats[None, None], roots[None, None])


def solution(mesh):
    placed = (P("dp", "factor", None, None), P("dp", "factor", None, None), P())
    return jax.shard_map(
        local,
        mesh=mesh,
        in_specs=placed,
        out_specs=(P("dp", "factor", None, None), P("dp", "factor", None, None)),
        check_vma=False,
    )
```
